256 devices in a mesh: ctx: 16 (over z, core), fsdp: 8 (over y_lo, x), tp: 2 (over y_hi).
Axes of the slice: x: 4, y: 4 (y_hi: 2, y_lo: 2; y = y_hi * 2 + y_lo), z: 8, core: 2. Of those that a mesh axis runs over, the one named last changes fastest.
Arguments:
- latents: bfloat16 [8, 4096, 5120], P('fsdp', 'ctx'), may hold values from -6 to 6
- queries: bfloat16 [8, 4096, 2560], P('fsdp', 'ctx', 'tp'), may hold values from -20 to 20
- grad_out: bfloat16 [8, 4096, 2560], P('fsdp', 'ctx', 'tp'), may hold values from -6 to 6
- key_weight: bfloat16 [5120, 512], P('fsdp', 'tp'), may hold values from -0.078125 to 0.078125
- value_weight: bfloat16 [5120, 512], P('fsdp', 'tp'), may hold values from -0.078125 to 0.078125
- block_order: int32 [32], replicated, may hold values from 0 to 31, each once
Outputs:
- grad_latents: bfloat16 [8, 4096, 5120], P('fsdp', 'ctx', 'tp')
- grad_key_weight: float32 [5120, 512], P('fsdp', 'tp')
- grad_value_weight: float32 [5120, 512], P('fsdp', 'tp')
The draws below stay inside these ranges and needn't reach their ends.
All inputs are finite; a program needn't handle non-finite values.
Results may differ from the reference program's by a relative error of at most 0.014.
The reference program's roundings to bfloat16 on the way (of `score_grad`) count: a program that leaves them out, or rounds other values in their place, can miss the bound.
Values may be sent and summed in bfloat16 or wider, within the bound.
No kernel may reach another device: no remote copies, remote signals or barrier semaphores. Data moves between devices by JAX's collectives and lax.ppermute only.
A program may use at most 128 MiB of HBM per device.

```python
import jax
import jax.numpy as jnp
from jax import lax

D = 5120
HD = 128
KVH = 4
QPG = 5
HQ = 20
L = 4096
BLK = 128
BLOCKS = 32
DOCS = 8


def draw_queries(key, part):
    key = jax.random.fold_in(key, 11)
    shape = (DOCS, L, HQ * HD)
    values = jax.random.truncated_normal(key, -6.0, 6.0, shape, jnp.float32)
    return values.astype(jnp.bfloat16)


def steps_of(stream_key, dims, cuts, smallest, top_value):
    level = 1.0
    for position, blocks in cuts:
        steps = jax.random.uniform(jax.random.fold_in(jax.random.fold_in(stream_key, 6), position), (blocks,), jnp.float32, smallest / len(cuts), top_value / len(cuts))
        level = level * jnp.repeat(jnp.exp(steps), dims[position] // blocks).reshape((-1,) + (1,) * (len(dims) - 1 - position))
    return level


def noise(rng, dims, width, reach, shards=(), kind=jnp.bfloat16):
    gain = steps_of(rng, dims, shards, -0.22, 0.18) if shards else 1.0
    array = jax.random.normal(rng, dims, jnp.float32) * width * gain
    return jnp.minimum(jnp.maximum(array, -reach), reach).astype(kind)


def setup_inputs(seed: int = 0) -> dict:
    splits = jax.random.split(jax.random.key(seed), 7)
    latents = noise(splits[0], (DOCS, L, D), 1.0, 6.0, ((0, 8), (1, 16)))
    queries = draw_queries(jax.random.fold_in(splits[6], 71), 0)
    grad_out = noise(splits[2], (DOCS, L, HQ * HD), 1.0, 6.0, ((0, 8), (1, 16), (2, 2)))
    key_weight = noise(splits[3], (D, KVH * HD), D ** -0.5, 0.078125, ((0, 8), (1, 2)))
    value_weight = noise(splits[4], (D, KVH * HD), D ** -0.5, 0.078125, ((0, 8), (1, 2)))
    block_order = jax.random.permutation(splits[5], BLOCKS).astype(jnp.int32)
    return {"latents": latents, "queries": queries, "grad_out": grad_out, "key_weight": key_weight, "value_weight": value_weight, "block_order": block_order}


def head_terms(head, keys, values, queries, grad_out, visible):
    group = head // QPG
    query_head = lax.dynamic_slice_in_dim(queries, head * HD, HD, 1)
    grad_head = lax.dynamic_slice_in_dim(grad_out, head * HD, HD, 1)
    key_head = lax.dynamic_slice_in_dim(keys, group * HD, HD, 1)
    value_head = lax.dynamic_slice_in_dim(values, group * HD, HD, 1)
    scale_factor = jnp.float32(HD ** -0.5)
    logits = jnp.dot(query_head, key_head.T, preferred_element_type=jnp.float32) * scale_factor
    row_max = jnp.max(jnp.where(visible, logits, jnp.float32(-1e30)), axis=1)
    weights = jnp.where(visible, jnp.exp(logits - row_max[:, None]), jnp.float32(0.0))
    row_total = jnp.sum(weights, axis=1)
    prob_grad = jnp.dot(grad_head, value_head.T, preferred_element_type=jnp.float32)
    delta = jnp.sum(weights * prob_grad, axis=1) / row_total
    lse = row_max + jnp.log(row_total)
    softmax = jnp.where(visible, jnp.exp(logits - lse[:, None]), jnp.float32(0.0))
    value_grad = jnp.dot(softmax.astype(jnp.bfloat16).T, grad_head, preferred_element_type=jnp.float32)
    score_grad = (softmax * (prob_grad - delta[:, None]) * scale_factor).astype(jnp.bfloat16)
    key_grad = jnp.dot(score_grad.T, query_head, preferred_element_type=jnp.float32)
    return key_grad, value_grad


def reference(latents, queries, grad_out, key_weight, value_weight, block_order):
    rows = jnp.arange(L, dtype=jnp.int32)
    positions = block_order[rows // BLK] * BLK + rows % BLK
    visible = positions[None, :] <= positions[:, None]

    def one_document(items):
        inputs, doc_queries, doc_grads = items
        keys = jnp.dot(inputs, key_weight, preferred_element_type=jnp.float32).astype(jnp.bfloat16)
        values = jnp.dot(inputs, value_weight, preferred_element_type=jnp.float32).astype(jnp.bfloat16)

        def per_head(head):
            return head_terms(head, keys, values, doc_queries, doc_grads, visible)

        key_parts, value_parts = lax.map(per_head, jnp.arange(HQ, dtype=jnp.int32))
        key_grads = jnp.sum(key_parts.reshape(KVH, QPG, L, HD), axis=1)
        value_grads = jnp.sum(value_parts.reshape(KVH, QPG, L, HD), axis=1)
        key_grads = jnp.transpose(key_grads, (1, 0, 2)).reshape(L, KVH * HD).astype(jnp.bfloat16)
        value_grads = jnp.transpose(value_grads, (1, 0, 2)).reshape(L, KVH * HD).astype(jnp.bfloat16)
        input_grad = jnp.dot(key_grads, key_weight.T, preferred_element_type=jnp.float32)
        input_grad = input_grad + jnp.dot(value_grads, value_weight.T, preferred_element_type=jnp.float32)
        key_wgrad = jnp.dot(inputs.T, key_grads, preferred_element_type=jnp.float32)
        value_wgrad = jnp.dot(inputs.T, value_grads, preferred_element_type=jnp.float32)
        return input_grad.astype(jnp.bfloat16), key_wgrad, value_wgrad

    grad_latents, key_wgrads, value_wgrads = lax.map(one_document, (latents, queries, grad_out))
    return grad_latents, jnp.sum(key_wgrads, axis=0), jnp.sum(value_wgrads, axis=0)
```

```python
import math
from functools import partial

import jax
import jax.numpy as jnp
from jax import lax
from jax.experimental import pallas as pl
from jax.experimental.pallas import tpu as pltpu
from jax.sharding import Mesh, PartitionSpec as P

HD = 128
QPG = 5
BLK = 128
WIDE = QPG * BLK
SCALE = HD**-0.5
SCALE2 = SCALE * math.log2(math.e)
LOW = -1e30

F32 = jnp.float32
BF16 = jnp.bfloat16


def nn(a, b):
    return lax.dot_general(a, b, (((1,), (0,)), ((), ())), preferred_element_type=F32)


def causal_mask():
    row = lax.broadcasted_iota(jnp.int32, (BLK, WIDE), 0)
    col = lax.broadcasted_iota(jnp.int32, (BLK, WIDE), 1)
    return row <= col % BLK


def stats_kernel(rows, first, last, *refs):
    count = len(rows)
    qpos, kpos, q_t, g_t = refs[:4]
    segments = refs[4 : 4 + count]
    rest = refs[4 + count :]
    if first:
        before, rest = None, rest
    else:
        before, rest = rest[:3], rest[3:]
    if last:
        lse_ref, delta_ref, top, total, weighted = rest
    else:
        top, total, weighted = rest
    if first:
        top[...] = jnp.full(top.shape, LOW, F32)
        total[...] = jnp.zeros(total.shape, F32)
        weighted[...] = jnp.zeros(weighted.shape, F32)
    else:
        top[...] = before[0][...]
        total[...] = before[1][...]
        weighted[...] = before[2][...]

    def add(seg, kb, qb, diagonal):
        start = pl.multiple_of(kb * BLK, BLK)
        logits = nn(seg[pl.ds(start, BLK), :HD], q_t[qb])
        prob_grad = nn(seg[pl.ds(start, BLK), HD:], g_t[qb])
        if diagonal:
            seen = causal_mask()
            logits = jnp.where(seen, logits, LOW)
        logits = logits.reshape(BLK // 8, 8, WIDE)
        prob_grad = prob_grad.reshape(BLK // 8, 8, WIDE)
        old = top[qb]
        new = jnp.maximum(old, jnp.max(logits, axis=0))
        weights = jnp.exp2(logits * SCALE2 - (new * SCALE2)[None])
        if diagonal:
            weights = jnp.where(seen.reshape(BLK // 8, 8, WIDE), weights, 0.0)
        rescale = jnp.exp2((old - new) * SCALE2)
        top[qb] = new
        total[qb] = total[qb] * rescale + jnp.sum(weights, axis=0)
        weighted[qb] = weighted[qb] * rescale + jnp.sum(weights * prob_grad, axis=0)

    base = 0
    for seg, height in zip(segments, rows):
        blocks = height // BLK

        def step(index, carry, seg=seg, base=base):
            kb, qb = index // 4, index % 4
            key_at, query_at = kpos[base + kb], qpos[qb]

            @pl.when(key_at < query_at)
            def _():
                add(seg, kb, qb, False)

            if first:

                @pl.when(key_at == query_at)
                def _():
                    add(seg, kb, qb, True)

            return carry

        lax.fori_loop(0, blocks * 4, step, 0)
        base += blocks
    if last:
        for qb in range(4):
            peak = jnp.max(top[qb], axis=0, keepdims=True)
            factor = jnp.exp2((top[qb] - peak) * SCALE2)
            full = jnp.sum(total[qb] * factor, axis=0, keepdims=True)
            lse_ref[qb] = peak * SCALE2 + jnp.log2(full)
            delta_ref[qb] = jnp.sum(weighted[qb] * factor, axis=0, keepdims=True) / full


def grads_kernel(rows, diagonal_too, *refs):
    count = len(rows)
    qpos, kpos, q_t, g_t, q_n, g_n, lse_ref, delta_ref = refs[:8]
    segments = refs[8 : 8 + count]
    outs = refs[8 + count :]

    def add(seg, out, kb, qb, diagonal):
        start = pl.multiple_of(kb * BLK, BLK)
        logits = nn(seg[pl.ds(start, BLK), :HD], q_t[qb])
        prob_grad = nn(seg[pl.ds(start, BLK), HD:], g_t[qb])
        softmax = jnp.exp2(logits * SCALE2 - lse_ref[qb])
        if diagonal:
            softmax = jnp.where(causal_mask(), softmax, 0.0)
        score_grad = (softmax * (prob_grad - delta_ref[qb]) * SCALE).astype(BF16)
        out[pl.ds(start, BLK), :HD] += nn(score_grad, q_n[qb])
        out[pl.ds(start, BLK), HD:] += nn(softmax.astype(BF16), g_n[qb])

    base = 0
    for seg, out, height in zip(segments, outs, rows):
        blocks = height // BLK
        out[...] = jnp.zeros(out.shape, F32)

        def step(index, carry, seg=seg, out=out, base=base):
            kb, qb = index // 4, index % 4
            key_at, query_at = kpos[base + kb], qpos[qb]

            @pl.when(key_at < query_at)
            def _():
                add(seg, out, kb, qb, False)

            if diagonal_too:

                @pl.when(key_at == query_at)
                def _():
                    add(seg, out, kb, qb, True)

            return carry

        lax.fori_loop(0, blocks * 4, step, 0)
        base += blocks


def smem():
    return pl.BlockSpec(memory_space=pltpu.SMEM)


def vmem():
    return pl.BlockSpec(memory_space=pltpu.VMEM)


def call(kernel, ins, out_shapes, flops, transcendentals, name):
    return pl.pallas_call(
        kernel,
        out_shape=out_shapes,
        in_specs=[smem(), smem()] + [vmem()] * (len(ins) - 2),
        out_specs=[vmem()] * len(out_shapes),
        compiler_params=pltpu.CompilerParams(vmem_limit_bytes=48 * 1024 * 1024),
        cost_estimate=pl.CostEstimate(
            flops=flops,
            bytes_accessed=sum(x.size * x.dtype.itemsize for x in ins),
            transcendentals=transcendentals,
        ),
        name=name,
    )(*ins)


def row_stats(qpos, kpos, q_t, g_t, segments, before, last):
    first = before is None
    rows = tuple(s.shape[0] for s in segments)
    stat = jax.ShapeDtypeStruct((4, 8, WIDE), F32)
    line = jax.ShapeDtypeStruct((4, 1, WIDE), F32)
    outs = ([line, line] if last else []) + [stat] * 3
    ins = [qpos, kpos, q_t, g_t, *segments] + ([] if first else list(before))
    pairs = sum(rows) // BLK * 4
    return call(
        partial(stats_kernel, rows, first, last),
        ins,
        outs,
        pairs * 2 * 4 * BLK * WIDE * HD,
        pairs * BLK * WIDE,
        "row_stats",
    )


def kv_grads(qpos, kpos, q_t, g_t, q_n, g_n, lse, delta, segments, diagonal_too):
    rows = tuple(s.shape[0] for s in segments)
    outs = [jax.ShapeDtypeStruct(s.shape, F32) for s in segments]
    pairs = sum(rows) // BLK * 4
    return call(
        partial(grads_kernel, rows, diagonal_too),
        [qpos, kpos, q_t, g_t, q_n, g_n, lse, delta, *segments],
        outs,
        pairs * 4 * 4 * BLK * WIDE * HD,
        pairs * BLK * WIDE,
        "kv_grads",
    )


def shift(value, axes, count, by):
    return lax.ppermute(value, axes, [(i, (i + by) % count) for i in range(count)])


def swap(value, axis):
    return lax.ppermute(value, axis, [(0, 1), (1, 0)])


def columns(value, start, width):
    return lax.dynamic_slice_in_dim(value, start, width, 1)


def after(value, *others):
    return lax.optimization_barrier((value, *others))[0]


def rotated(parts, start):
    both = jnp.concatenate(parts + parts[:-1], axis=0)
    size = parts[0].shape[0]
    return lax.dynamic_slice_in_dim(both, start * size, size * len(parts), 0)


def per_device(latents, queries, grad_out, key_weight, value_weight, block_order):
    own_rows = latents[0]
    half = own_rows.shape[0]
    planes = lax.axis_size("z")
    docs = lax.axis_size("yl") * lax.axis_size("x")
    fsdp = ("yl", "x")
    core = lax.axis_index("c")
    plane = lax.axis_index("z")
    group = lax.axis_index("t")
    place = lax.axis_index("yl") * lax.axis_size("x") + lax.axis_index("x")
    depth = key_weight.shape[0]
    width = own_rows.shape[1]

    def head_part(value, which):
        return columns(value, which * WIDE, WIDE)

    weight = jnp.concatenate(
        [columns(key_weight, core * HD, HD), columns(value_weight, core * HD, HD)], axis=1
    )
    weights = [weight] + [shift(weight, fsdp, docs, k) for k in range(1, docs)]
    other_rows = swap(own_rows, "c")
    query_rows = [head_part(queries[0], core), swap(head_part(queries[0], 1 - core), "c")]
    grad_rows = [head_part(grad_out[0], core), swap(head_part(grad_out[0], 1 - core), "c")]

    def by_block(pair):
        stacked = jnp.concatenate(pair, axis=0).reshape(4, BLK, QPG, HD)
        natural = stacked.transpose(0, 2, 1, 3).reshape(4, WIDE, HD)
        turned = stacked.transpose(0, 3, 2, 1).reshape(4, HD, WIDE)
        return natural, turned

    q_n, q_t = by_block(query_rows)
    g_n, g_t = by_block(grad_rows)

    def block_places(plane_index):
        first = plane_index % planes * 4
        mine = lax.dynamic_slice_in_dim(block_order, first + 2 * core, 2)
        others = lax.dynamic_slice_in_dim(block_order, first + 2 * (1 - core), 2)
        return jnp.concatenate([mine, others])

    qpos = block_places(plane)

    rows = jnp.concatenate([own_rows, other_rows], axis=0)
    total = None
    for k in range(docs):
        source = (place + docs - k) % docs
        term = nn(columns(rows, source * depth, depth), weights[k])
        total = term if total is None else total + term
    kv = total.astype(BF16)

    rights, lefts = [kv], [kv]
    for k in range(1, 4):
        rights.append(shift(rights[-1], "z", planes, 1))
        lefts.append(shift(lefts[-1], "z", planes, -1))
    rights.append(shift(rights[-1][:half], "z", planes, 1))
    lefts.append(shift(lefts[-1][half:], "z", planes, -1))
    left_pos = [block_places(plane + k) for k in range(5)]
    right_pos = [block_places(plane + planes - k) for k in range(5)]
    far_pos = left_pos[4]

    state = row_stats(qpos, qpos, q_t, g_t, [kv], None, False)
    for k in range(1, 4):
        kpos = jnp.concatenate([left_pos[k], right_pos[k]])
        state = row_stats(qpos, kpos, q_t, g_t, [lefts[k], rights[k]], state, False)
    lse, delta, *_ = row_stats(qpos, far_pos, q_t, g_t, [rights[4], lefts[4]], state, True)

    held = after(own_rows, kv)
    pieces = [
        shift(columns(held, (place + k) % docs * depth, depth), fsdp, docs, k)
        for k in range(1, docs)
    ]
    other_pieces = swap(jnp.concatenate(pieces, axis=0), "c")
    latent_parts = [columns(rows, place * depth, depth)] + [
        jnp.concatenate([p, other_pieces[i * half : (i + 1) * half]], axis=0)
        for i, p in enumerate(pieces)
    ]
    full_weight = rotated(weights[::-1], docs - 1 - place)
    other_weight = swap(after(full_weight, kv), "c")

    grads = partial(kv_grads, qpos, q_t=q_t, g_t=g_t, q_n=q_n, g_n=g_n, lse=lse, delta=delta)
    far_right, far_left = grads(far_pos, segments=[rights[4], lefts[4]], diagonal_too=False)
    to_right = shift(far_right.astype(BF16), "z", planes, 1)
    to_left = shift(far_left.astype(BF16), "z", planes, -1)
    for k in range(3, 0, -1):
        kpos = jnp.concatenate([left_pos[k], right_pos[k]])
        ahead, behind = grads(kpos, segments=[lefts[k], rights[k]], diagonal_too=False)
        if k == 3:
            ahead = jnp.concatenate([ahead[:half] + to_right.astype(F32), ahead[half:]], axis=0)
            behind = jnp.concatenate([behind[:half], behind[half:] + to_left.astype(F32)], axis=0)
        else:
            ahead = ahead + to_right.astype(F32)
            behind = behind + to_left.astype(F32)
        to_right = shift(ahead.astype(BF16), "z", planes, 1)
        to_left = shift(behind.astype(BF16), "z", planes, -1)
    (here,) = grads(qpos, segments=[kv], diagonal_too=True)
    grad_kv = (here + to_right.astype(F32) + to_left.astype(F32)).astype(BF16)

    gathered = [grad_kv] + [shift(grad_kv, fsdp, docs, k) for k in range(1, docs)]
    weight_grad = None
    for part, grad in zip(latent_parts, gathered):
        term = lax.dot_general(part, grad, (((0,), (0,)), ((), ())), preferred_element_type=F32)
        weight_grad = term if weight_grad is None else weight_grad + term
    cut = depth // planes
    spread = lax.all_to_all(
        weight_grad.astype(BF16).reshape(planes, cut, 2 * HD), "z", 0, 0, tiled=True
    )
    summed = jnp.sum(spread.astype(F32), axis=0).astype(BF16)
    ring = [summed] + [shift(summed, "z", planes, k) for k in range(1, planes)]
    mine = rotated(ring[::-1], planes - 1 - plane)
    theirs = swap(mine, "c")
    low = jnp.where(core == 0, mine, theirs).astype(F32)
    high = jnp.where(core == 0, theirs, mine).astype(F32)
    key_out = jnp.concatenate([low[:, :HD], high[:, :HD]], axis=1)
    value_out = jnp.concatenate([low[:, HD:], high[:, HD:]], axis=1)

    grad_own = grad_kv[:half]
    grad_other = swap(grad_kv[half:], "c")

    def input_term(which):
        def half_of(value):
            return lax.dynamic_slice_in_dim(value, which * (width // 2), width // 2, 0)

        contract = (((1,), (1,)), ((), ()))
        return lax.dot_general(
            grad_own, half_of(full_weight), contract, preferred_element_type=F32
        ) + lax.dot_general(
            grad_other, half_of(other_weight), contract, preferred_element_type=F32
        )

    arrived = swap(input_term(1 - group).astype(BF16), "t")
    grad_inputs = (input_term(group) + arrived.astype(F32)).astype(BF16)
    return grad_inputs[None], key_out, value_out


def solution(mesh):
    sizes = mesh.shape
    ctx, fsdp, tp = sizes["ctx"], sizes["fsdp"], sizes["tp"]
    fine = Mesh(
        mesh.devices.reshape(ctx // 2, 2, 2, fsdp // 2, tp), ("z", "c", "yl", "x", "t")
    )
    rows, cols = ("z", "c"), ("yl", "x")
    placed = (
        P(cols, rows, None),
        P(cols, rows, "t"),
        P(cols, rows, "t"),
        P(cols, "t"),
        P(cols, "t"),
        P(),
    )
    return jax.shard_map(
        per_device,
        mesh=fine,
        in_specs=placed,
        out_specs=(P(cols, rows, "t"), P(cols, "t"), P(cols, "t")),
        check_vma=False,
    )
```

```python
import math
from functools import partial

import jax
import jax.numpy as jnp
from jax import lax
from jax.experimental import pallas as pl
from jax.experimental.pallas import tpu as pltpu
from jax.sharding import Mesh, PartitionSpec as P

HD = 128
QPG = 5
BLK = 128
WIDE = QPG * BLK
SCALE = HD**-0.5
SCALE2 = SCALE * math.log2(math.e)
LOW = -1e30

F32 = jnp.float32
BF16 = jnp.bfloat16


def nn(a, b):
    return lax.dot_general(a, b, (((1,), (0,)), ((), ())), preferred_element_type=F32)


def dot_tn(a, b):
    return lax.dot_general(a, b, (((0,), (0,)), ((), ())), preferred_element_type=F32)


def causal_mask():
    row = lax.broadcasted_iota(jnp.int32, (BLK, WIDE), 0)
    col = lax.broadcasted_iota(jnp.int32, (BLK, WIDE), 1)
    return row <= col % BLK


def block_at(index):
    return pl.ds(pl.multiple_of(index * BLK, BLK), BLK)


def gather_segments(segments, held):
    base = 0
    for seg in segments:
        held[base : base + seg.shape[0], :] = seg[...]
        base += seg.shape[0]


def rows_of(held, blocks, first):
    parts = [held[block_at(b), first : first + HD] for b in blocks]
    return parts[0] if len(parts) == 1 else jnp.concatenate(parts, axis=0)


def walk(counts, order, stage, qb, add):
    visible = counts[stage, qb]
    fours = visible // 4
    left = visible - fours * 4

    def step(i, carry):
        add([order[stage, i * 4 + j] for j in range(4)])
        return carry

    lax.fori_loop(0, fours, step, 0)

    @pl.when(left >= 2)
    def _():
        add([order[stage, fours * 4 + j] for j in range(2)])

    @pl.when(left % 2 == 1)
    def _():
        add([order[stage, visible - 1]])


def stats_kernel(stage, count, last, *refs):
    counts, order, q_t, g_t = refs[:4]
    segments = refs[4 : 4 + count]
    rest = refs[4 + count :]
    held = rest[-1]
    first = stage == 0
    before, rest = (None, rest[:-1]) if first else (rest[:3], rest[3:-1])
    top, total, weighted = rest[-3:]
    gather_segments(segments, held)
    for i, fill in enumerate((LOW, 0.0, 0.0)):
        ref = rest[len(rest) - 3 + i]
        ref[...] = jnp.full(ref.shape, fill, F32) if first else before[i][...]

    for qb in range(4):

        def add(blocks, diagonal=False, qb=qb):
            deep = len(blocks) * BLK // 8
            logits = nn(rows_of(held, blocks, 0), q_t[qb])
            prob_grad = nn(rows_of(held, blocks, HD), g_t[qb])
            if diagonal:
                seen = causal_mask()
                logits = jnp.where(seen, logits, LOW)
            logits = logits.reshape(deep, 8, WIDE)
            prob_grad = prob_grad.reshape(deep, 8, WIDE)
            old = top[qb]
            new = jnp.maximum(old, jnp.max(logits, axis=0))
            weights = jnp.exp2(logits * SCALE2 - (new * SCALE2)[None])
            if diagonal:
                weights = jnp.where(seen.reshape(deep, 8, WIDE), weights, 0.0)
            rescale = jnp.exp2((old - new) * SCALE2)
            top[qb] = new
            total[qb] = total[qb] * rescale + jnp.sum(weights, axis=0)
            weighted[qb] = weighted[qb] * rescale + jnp.sum(weights * prob_grad, axis=0)

        walk(counts, order, stage, qb, add)
        if first:
            add([qb], True)
        if last:
            lse_ref, delta_ref = rest[:2]
            peak = jnp.max(top[qb], axis=0, keepdims=True)
            factor = jnp.exp2((top[qb] - peak) * SCALE2)
            full = jnp.sum(total[qb] * factor, axis=0, keepdims=True)
            lse_ref[qb] = peak * SCALE2 + jnp.log2(full)
            delta_ref[qb] = jnp.sum(weighted[qb] * factor, axis=0, keepdims=True) / full


def grads_kernel(stage, count, *refs):
    counts, order, q_t, g_t, q_n, g_n, lse_ref, delta_ref = refs[:8]
    segments = refs[8 : 8 + count]
    out, held = refs[8 + count :]
    gather_segments(segments, held)
    out[...] = jnp.zeros(out.shape, F32)

    for qb in range(4):

        def add(blocks, diagonal=False, qb=qb):
            logits = nn(rows_of(held, blocks, 0), q_t[qb])
            prob_grad = nn(rows_of(held, blocks, HD), g_t[qb])
            softmax = jnp.exp2(logits * SCALE2 - lse_ref[qb])
            if diagonal:
                softmax = jnp.where(causal_mask(), softmax, 0.0)
            score_grad = (softmax * (prob_grad - delta_ref[qb])).astype(BF16)
            key_grad = nn(score_grad, q_n[qb]) * SCALE
            value_grad = nn(softmax.astype(BF16), g_n[qb])
            for i, b in enumerate(blocks):
                out[block_at(b), :HD] += key_grad[i * BLK : (i + 1) * BLK]
                out[block_at(b), HD:] += value_grad[i * BLK : (i + 1) * BLK]

        walk(counts, order, stage, qb, add)
        if stage == 0:
            add([qb], True)


def smem():
    return pl.BlockSpec(memory_space=pltpu.SMEM)


def vmem():
    return pl.BlockSpec(memory_space=pltpu.VMEM)


def call(kernel, ins, out_shapes, rows, products, name):
    pairs = rows // BLK * 4 // 2
    return pl.pallas_call(
        kernel,
        out_shape=out_shapes,
        in_specs=[smem(), smem()] + [vmem()] * (len(ins) - 2),
        out_specs=[vmem()] * len(out_shapes),
        scratch_shapes=[pltpu.VMEM((rows, 2 * HD), BF16)],
        compiler_params=pltpu.CompilerParams(vmem_limit_bytes=48 * 1024 * 1024),
        cost_estimate=pl.CostEstimate(
            flops=pairs * products * 4 * BLK * WIDE * HD,
            bytes_accessed=sum(x.size * x.dtype.itemsize for x in ins),
            transcendentals=pairs * BLK * WIDE,
        ),
        name=name,
    )(*ins)


def row_stats(stage, plan, q_t, g_t, segments, before, last):
    stat = jax.ShapeDtypeStruct((4, 8, WIDE), F32)
    line = jax.ShapeDtypeStruct((4, 1, WIDE), F32)
    return call(
        partial(stats_kernel, stage, len(segments), last),
        [*plan, q_t, g_t, *segments, *before],
        ([line, line] if last else []) + [stat] * 3,
        sum(s.shape[0] for s in segments),
        2,
        "row_stats",
    )


def kv_grads(stage, segments, plan, q_t, g_t, q_n, g_n, lse, delta):
    rows = sum(s.shape[0] for s in segments)
    (out,) = call(
        partial(grads_kernel, stage, len(segments)),
        [*plan, q_t, g_t, q_n, g_n, lse, delta, *segments],
        [jax.ShapeDtypeStruct((rows, 2 * HD), F32)],
        rows,
        4,
        "kv_grads",
    )
    return out


def weight_kernel(place_ref, own, other, *refs):
    gathered, out = refs[:-1], refs[-1]
    span = len(gathered)
    half = gathered[0].shape[0] // 2
    for k, grad in enumerate(gathered):
        source = lax.rem(place_ref[0] + span - k, span)
        term = dot_tn(own[source, 0], grad[:half, :]) + dot_tn(other[source, 0], grad[half:, :])
        if k == 0:
            out[...] = term
        else:
            out[...] += term


def weight_grads(place, which, own, other, gathered):
    span = len(gathered)
    half = gathered[0].shape[0] // 2
    depth = own.shape[1]
    own = own.reshape(span, 2, half, depth)
    other = other.reshape(span, 2, half, depth)
    part = pl.BlockSpec((span, 1, half, depth), lambda i: (0, which, 0, 0))
    grad = pl.BlockSpec(gathered[0].shape, lambda i: (0, 0))
    return pl.pallas_call(
        weight_kernel,
        grid=(1,),
        out_shape=jax.ShapeDtypeStruct((depth, 2 * HD), F32),
        in_specs=[smem(), part, part] + [grad] * span,
        out_specs=pl.BlockSpec((depth, 2 * HD), lambda i: (0, 0)),
        compiler_params=pltpu.CompilerParams(vmem_limit_bytes=48 * 1024 * 1024),
        cost_estimate=pl.CostEstimate(
            flops=4 * span * half * depth * 2 * HD,
            bytes_accessed=4 * span * half * depth,
            transcendentals=0,
        ),
        name="weight_grads",
    )(place, own, other, *gathered)


def shift(value, axes, count, by):
    return lax.ppermute(value, axes, [(i, (i + by) % count) for i in range(count)])


def swap(value, axis):
    return lax.ppermute(value, axis, [(0, 1), (1, 0)])


def columns(value, start, width):
    return lax.dynamic_slice_in_dim(value, start, width, 1)


def after(value, *others):
    return lax.optimization_barrier((value, *others))[0]


def pick(parts, index):
    chosen = parts[0]
    for i in range(1, len(parts)):
        chosen = jnp.where(index == i, parts[i], chosen)
    return chosen


def dot_nt(a, b):
    return lax.dot_general(a, b, (((1,), (1,)), ((), ())), preferred_element_type=F32)


def per_device(latents, queries, grad_out, key_weight, value_weight, block_order):
    own_rows = latents[0]
    half = own_rows.shape[0]
    planes = lax.axis_size("z")
    span = lax.axis_size("x")
    core = lax.axis_index("c")
    plane = lax.axis_index("z")
    group = lax.axis_index("t")
    side = lax.axis_index("yl")
    place = lax.axis_index("x")
    depth = key_weight.shape[0]
    stretch = depth * span

    def head_part(value, which):
        return columns(value, which * WIDE, WIDE)

    weight = jnp.concatenate(
        [columns(key_weight, core * HD, HD), columns(value_weight, core * HD, HD)], axis=1
    )
    near, far = [weight] * span, [weight] * span
    for k in (2, 1, 3):
        near[k] = shift(weight, "x", span, k)
    far[0] = swap(weight, "yl")
    other_rows = swap(own_rows, "c")
    passed, crossing, *_ = lax.optimization_barrier(
        (far[0], near[2], other_rows, queries[0], grad_out[0])
    )
    queries, grad_out = _[1:]
    other_rows = _[0]
    query_rows = [head_part(queries, core), swap(head_part(queries, 1 - core), "c")]
    grad_rows = [head_part(grad_out, core), swap(head_part(grad_out, 1 - core), "c")]
    far[1] = shift(passed, "x", span, 1)
    far[3] = shift(passed, "x", span, 3)
    far[2] = swap(crossing, "yl")

    def by_block(pair):
        stacked = jnp.concatenate(pair, axis=0).reshape(4, BLK, QPG, HD)
        natural = stacked.transpose(0, 2, 1, 3).reshape(4, WIDE, HD)
        turned = stacked.transpose(0, 3, 2, 1).reshape(4, HD, WIDE)
        return natural, turned

    q_n, q_t = by_block(query_rows)
    g_n, g_t = by_block(grad_rows)

    def block_places(plane_index):
        first = plane_index % planes * 4
        mine = lax.dynamic_slice_in_dim(block_order, first + 2 * core, 2)
        others = lax.dynamic_slice_in_dim(block_order, first + 2 * (1 - core), 2)
        return jnp.concatenate([mine, others])

    qpos = block_places(plane)
    none = jnp.full((4,), 1 << 20, jnp.int32)
    kpos = jnp.stack(
        [jnp.concatenate([qpos, none])]
        + [
            jnp.concatenate([block_places(plane + k), block_places(plane + planes - k)])
            for k in range(1, 4)
        ]
        + [jnp.concatenate([block_places(plane + 4), none])]
    )
    ids = jnp.arange(8, dtype=jnp.int32)
    mine_at, other_at = kpos[:, :, None], kpos[:, None, :]
    lower = (other_at < mine_at) | ((other_at == mine_at) & (ids[None, None, :] < ids[None, :, None]))
    rank = jnp.sum(lower.astype(jnp.int32), axis=2)
    order = jnp.sum(
        jnp.where(rank[:, :, None] == ids[None, None, :], ids[None, :, None], 0), axis=1
    )
    counts = jnp.sum((kpos[:, None, :] < qpos[None, :, None]).astype(jnp.int32), axis=2)
    plan = (counts, order)

    rows = jnp.concatenate([own_rows, other_rows], axis=0)
    total = None
    for here, parts, order in (
        (side, near, (0, 1, 3, 2)),
        (1 - side, far, (0, 1, 3, 2)),
    ):
        for k in order:
            source = here * span + (place + span - k) % span
            term = nn(columns(rows, source * depth, depth), parts[k])
            total = term if total is None else total + term
    kv = total.astype(BF16)

    rights, lefts = [kv], [kv]
    for k in range(1, 4):
        rights.append(shift(rights[-1], "z", planes, 1))
        lefts.append(shift(lefts[-1], "z", planes, -1))
    rights.append(shift(rights[-1][:half], "z", planes, 1))
    lefts.append(shift(lefts[-1][half:], "z", planes, -1))

    state = row_stats(0, plan, q_t, g_t, [kv], [], False)
    for k in range(1, 4):
        state = row_stats(k, plan, q_t, g_t, [lefts[k], rights[k]], state, False)
        if k == 1:
            near_state = state
    lse, delta, *_ = row_stats(4, plan, q_t, g_t, [rights[4], lefts[4]], state, True)

    by_place = jnp.concatenate(
        [
            columns(own_rows, which * stretch + i * depth, depth)
            for i in range(span)
            for which in (1 - side, side)
        ],
        axis=0,
    )
    latents_x = lax.all_to_all(after(by_place, near_state[1]), "x", 0, 0, tiled=True)
    latents_other = swap(latents_x, "c")

    held = lax.optimization_barrier((*near, *far, lefts[2], rights[2]))

    def half_of(which):
        chosen = [
            jnp.where(which == side, a, b) for a, b in zip(held[:span], held[span : 2 * span])
        ]
        turned = [pick(chosen, (place + span - i) % span) for i in range(span)]
        return jnp.concatenate(turned, axis=0)

    mine_w = half_of(group)
    group_w = swap(half_of(1 - group), "t")
    mine_w, group_w, lse = lax.optimization_barrier((mine_w, group_w, lse))
    core_w, core_group_w = swap(mine_w, "c"), swap(group_w, "c")

    grads = partial(
        kv_grads, plan=plan, q_t=q_t, g_t=g_t, q_n=q_n, g_n=g_n, lse=lse, delta=delta
    )
    distant = grads(4, [rights[4], lefts[4]])
    to_right = shift(distant[:half].astype(BF16), "z", planes, 1)
    to_left = shift(distant[half:].astype(BF16), "z", planes, -1)
    for k in range(3, 0, -1):
        pair = grads(k, [lefts[k], rights[k]])
        ahead, behind = pair[: 2 * half], pair[2 * half :]
        if k == 3:
            ahead = jnp.concatenate([ahead[:half] + to_right.astype(F32), ahead[half:]], axis=0)
            behind = jnp.concatenate([behind[:half], behind[half:] + to_left.astype(F32)], axis=0)
        else:
            ahead = ahead + to_right.astype(F32)
            behind = behind + to_left.astype(F32)
        to_right = shift(ahead.astype(BF16), "z", planes, 1)
        to_left = shift(behind.astype(BF16), "z", planes, -1)
    kv_last, latents_x, latents_other, core_w, core_group_w = lax.optimization_barrier(
        (kv, latents_x, latents_other, core_w, core_group_w)
    )
    here = grads(0, [kv_last])
    grad_kv = (here + to_right.astype(F32) + to_left.astype(F32)).astype(BF16)

    gathered = [grad_kv] + [shift(grad_kv, "x", span, k) for k in range(1, span)]
    grad_group = swap(grad_kv, "t")

    def weight_term(which):
        return weight_grads(
            jnp.reshape(place, (1,)), which, latents_x, latents_other, gathered
        )

    crossed = swap(weight_term(0).astype(BF16), "yl")
    weight_grad = (weight_term(1) + crossed.astype(F32)).astype(BF16)
    cut = depth // planes
    spread = lax.all_to_all(weight_grad.reshape(planes, cut, 2 * HD), "z", 0, 0, tiled=True)
    summed = jnp.sum(spread.astype(F32), axis=0).astype(BF16)
    copies = jnp.broadcast_to(summed[None], (2 * planes, cut, 2 * HD))
    whole = lax.all_to_all(copies, ("z", "c"), 0, 0, tiled=True)
    whole = whole.reshape(planes, 2, cut, 2 * HD).transpose(0, 2, 1, 3).astype(F32)
    key_out = whole[..., :HD].reshape(depth, 2 * HD)
    value_out = whole[..., HD:].reshape(depth, 2 * HD)

    grad_core = swap(grad_kv[half:], "c")
    grad_core_group = swap(grad_group[half:], "c")
    grad_inputs = (
        dot_nt(grad_kv[:half], mine_w)
        + dot_nt(grad_core, core_w)
        + dot_nt(grad_group[:half], group_w)
        + dot_nt(grad_core_group, core_group_w)
    ).astype(BF16)
    return grad_inputs[None], key_out, value_out


def solution(mesh):
    sizes = mesh.shape
    ctx, fsdp, tp = sizes["ctx"], sizes["fsdp"], sizes["tp"]
    fine = Mesh(
        mesh.devices.reshape(ctx // 2, 2, 2, fsdp // 2, tp), ("z", "c", "yl", "x", "t")
    )
    rows, cols = ("z", "c"), ("yl", "x")
    placed = (
        P(cols, rows, None),
        P(cols, rows, "t"),
        P(cols, rows, "t"),
        P(cols, "t"),
        P(cols, "t"),
        P(),
    )
    return jax.shard_map(
        per_device,
        mesh=fine,
        in_specs=placed,
        out_specs=(P(cols, rows, "t"), P(cols, "t"), P(cols, "t")),
        check_vma=False,
    )
```

```python
import math
from functools import partial

import jax
import jax.numpy as jnp
from jax import lax
from jax.experimental import pallas as pl
from jax.experimental.pallas import tpu as pltpu
from jax.sharding import Mesh, PartitionSpec as P

HD = 128
QPG = 5
BLK = 128
WIDE = QPG * BLK
SCALE = HD**-0.5
SCALE2 = SCALE * math.log2(math.e)
LOW = -1e30
VMEM = 20 * 1024 * 1024

F32 = jnp.float32
BF16 = jnp.bfloat16


def nn(a, b):
    return lax.dot_general(a, b, (((1,), (0,)), ((), ())), preferred_element_type=F32)


def dot_tn(a, b):
    return lax.dot_general(a, b, (((0,), (0,)), ((), ())), preferred_element_type=F32)


def causal_mask():
    row = lax.broadcasted_iota(jnp.int32, (BLK, WIDE), 0)
    col = lax.broadcasted_iota(jnp.int32, (BLK, WIDE), 1)
    return row <= col % BLK


def block_at(index):
    return pl.ds(pl.multiple_of(index * BLK, BLK), BLK)


def gather_segments(segments, held):
    base = 0
    for seg in segments:
        held[base : base + seg.shape[0], :] = seg[...]
        base += seg.shape[0]


def rows_of(held, blocks, first):
    parts = [held[block_at(b), first : first + HD] for b in blocks]
    return parts[0] if len(parts) == 1 else jnp.concatenate(parts, axis=0)


def walk(counts, order, stage, qb, add):
    visible = counts[stage, qb]
    fours = visible // 4
    left = visible - fours * 4

    def step(i, carry):
        add([order[stage, i * 4 + j] for j in range(4)])
        return carry

    lax.fori_loop(0, fours, step, 0)

    @pl.when(left >= 2)
    def _():
        add([order[stage, fours * 4 + j] for j in range(2)])

    @pl.when(left % 2 == 1)
    def _():
        add([order[stage, visible - 1]])


def stats_kernel(stage, count, last, *refs):
    counts, order, q_t, g_t = refs[:4]
    segments = refs[4 : 4 + count]
    rest = refs[4 + count :]
    held = rest[-1]
    first = stage == 0
    before, rest = (None, rest[:-1]) if first else (rest[:3], rest[3:-1])
    top, total, weighted = rest[-3:]
    gather_segments(segments, held)
    for i, fill in enumerate((LOW, 0.0, 0.0)):
        ref = rest[len(rest) - 3 + i]
        ref[...] = jnp.full(ref.shape, fill, F32) if first else before[i][...]

    for qb in range(4):

        def add(blocks, diagonal=False, qb=qb):
            deep = len(blocks) * BLK // 8
            logits = nn(rows_of(held, blocks, 0), q_t[qb])
            prob_grad = nn(rows_of(held, blocks, HD), g_t[qb])
            if diagonal:
                seen = causal_mask()
                logits = jnp.where(seen, logits, LOW)
            logits = logits.reshape(deep, 8, WIDE)
            prob_grad = prob_grad.reshape(deep, 8, WIDE)
            old = top[qb]
            new = jnp.maximum(old, jnp.max(logits, axis=0))
            weights = jnp.exp2(logits * SCALE2 - (new * SCALE2)[None])
            if diagonal:
                weights = jnp.where(seen.reshape(deep, 8, WIDE), weights, 0.0)
            rescale = jnp.exp2((old - new) * SCALE2)
            top[qb] = new
            total[qb] = total[qb] * rescale + jnp.sum(weights, axis=0)
            weighted[qb] = weighted[qb] * rescale + jnp.sum(weights * prob_grad, axis=0)

        walk(counts, order, stage, qb, add)
        if first:
            add([qb], True)
        if last:
            lse_ref, delta_ref = rest[:2]
            peak = jnp.max(top[qb], axis=0, keepdims=True)
            factor = jnp.exp2((top[qb] - peak) * SCALE2)
            full = jnp.sum(total[qb] * factor, axis=0, keepdims=True)
            lse_ref[qb] = peak * SCALE2 + jnp.log2(full)
            delta_ref[qb] = jnp.sum(weighted[qb] * factor, axis=0, keepdims=True) / full


def grads_kernel(stage, count, *refs):
    counts, order, q_t, g_t, q_n, g_n, lse_ref, delta_ref = refs[:8]
    segments = refs[8 : 8 + count]
    out, held = refs[8 + count :]
    gather_segments(segments, held)
    out[...] = jnp.zeros(out.shape, F32)

    for qb in range(4):

        def add(blocks, diagonal=False, qb=qb):
            logits = nn(rows_of(held, blocks, 0), q_t[qb])
            prob_grad = nn(rows_of(held, blocks, HD), g_t[qb])
            softmax = jnp.exp2(logits * SCALE2 - lse_ref[qb])
            if diagonal:
                softmax = jnp.where(causal_mask(), softmax, 0.0)
            score_grad = (softmax * (prob_grad - delta_ref[qb])).astype(BF16)
            key_grad = nn(score_grad, q_n[qb]) * SCALE
            value_grad = nn(softmax.astype(BF16), g_n[qb])
            for i, b in enumerate(blocks):
                out[block_at(b), :HD] += key_grad[i * BLK : (i + 1) * BLK]
                out[block_at(b), HD:] += value_grad[i * BLK : (i + 1) * BLK]

        walk(counts, order, stage, qb, add)
        if stage == 0:
            add([qb], True)


def smem():
    return pl.BlockSpec(memory_space=pltpu.SMEM)


def vmem():
    return pl.BlockSpec(memory_space=pltpu.VMEM)


def call(kernel, ins, out_shapes, rows, products, name):
    pairs = rows // BLK * 4 // 2
    return pl.pallas_call(
        kernel,
        out_shape=out_shapes,
        in_specs=[smem(), smem()] + [vmem()] * (len(ins) - 2),
        out_specs=[vmem()] * len(out_shapes),
        scratch_shapes=[pltpu.VMEM((rows, 2 * HD), BF16)],
        compiler_params=pltpu.CompilerParams(vmem_limit_bytes=VMEM),
        cost_estimate=pl.CostEstimate(
            flops=pairs * products * 4 * BLK * WIDE * HD,
            bytes_accessed=sum(x.size * x.dtype.itemsize for x in ins),
            transcendentals=pairs * BLK * WIDE,
        ),
        name=name,
    )(*ins)


def row_stats(stage, plan, q_t, g_t, segments, before, last):
    stat = jax.ShapeDtypeStruct((4, 8, WIDE), F32)
    line = jax.ShapeDtypeStruct((4, 1, WIDE), F32)
    return call(
        partial(stats_kernel, stage, len(segments), last),
        [*plan, q_t, g_t, *segments, *before],
        ([line, line] if last else []) + [stat] * 3,
        sum(s.shape[0] for s in segments),
        2,
        "row_stats",
    )


def kv_grads(stage, segments, plan, q_t, g_t, q_n, g_n, lse, delta):
    rows = sum(s.shape[0] for s in segments)
    (out,) = call(
        partial(grads_kernel, stage, len(segments)),
        [*plan, q_t, g_t, q_n, g_n, lse, delta, *segments],
        [jax.ShapeDtypeStruct((rows, 2 * HD), F32)],
        rows,
        4,
        "kv_grads",
    )
    return out


def weight_kernel(place_ref, own, other, *refs):
    gathered, out = refs[:-1], refs[-1]
    span = len(gathered)
    half = gathered[0].shape[0] // 2
    for k, grad in enumerate(gathered):
        source = lax.rem(place_ref[0] + span - k, span)
        term = dot_tn(own[source, 0], grad[:half, :]) + dot_tn(other[source, 0], grad[half:, :])
        if k == 0:
            out[...] = term
        else:
            out[...] += term


def weight_grads(place, which, own, other, gathered):
    span = len(gathered)
    half = gathered[0].shape[0] // 2
    depth = own.shape[1]
    own = own.reshape(span, 2, half, depth)
    other = other.reshape(span, 2, half, depth)
    part = pl.BlockSpec((span, 1, half, depth), lambda i: (0, which, 0, 0))
    grad = pl.BlockSpec(gathered[0].shape, lambda i: (0, 0))
    return pl.pallas_call(
        weight_kernel,
        grid=(1,),
        out_shape=jax.ShapeDtypeStruct((depth, 2 * HD), F32),
        in_specs=[smem(), part, part] + [grad] * span,
        out_specs=pl.BlockSpec((depth, 2 * HD), lambda i: (0, 0)),
        compiler_params=pltpu.CompilerParams(vmem_limit_bytes=VMEM),
        cost_estimate=pl.CostEstimate(
            flops=4 * span * half * depth * 2 * HD,
            bytes_accessed=4 * span * half * depth,
            transcendentals=0,
        ),
        name="weight_grads",
    )(place, own, other, *gathered)


def shift(value, axes, count, by):
    return lax.ppermute(value, axes, [(i, (i + by) % count) for i in range(count)])


def swap(value, axis):
    return lax.ppermute(value, axis, [(0, 1), (1, 0)])


def columns(value, start, width):
    return lax.dynamic_slice_in_dim(value, start, width, 1)


def after(value, *others):
    return lax.optimization_barrier((value, *others))[0]


def pick(parts, index):
    chosen = parts[0]
    for i in range(1, len(parts)):
        chosen = jnp.where(index == i, parts[i], chosen)
    return chosen


def dot_nt(a, b):
    return lax.dot_general(a, b, (((1,), (1,)), ((), ())), preferred_element_type=F32)


def per_device(latents, queries, grad_out, key_weight, value_weight, block_order):
    own_rows = latents[0]
    half = own_rows.shape[0]
    planes = lax.axis_size("z")
    span = lax.axis_size("x")
    core = lax.axis_index("c")
    plane = lax.axis_index("z")
    group = lax.axis_index("t")
    side = lax.axis_index("yl")
    place = lax.axis_index("x")
    depth = key_weight.shape[0]
    stretch = depth * span

    def head_part(value, which):
        return columns(value, which * WIDE, WIDE)

    weight = jnp.concatenate(
        [columns(key_weight, core * HD, HD), columns(value_weight, core * HD, HD)], axis=1
    )
    near, far = [weight] * span, [weight] * span
    for k in (2, 1, 3):
        near[k] = shift(weight, "x", span, k)
    far[0] = swap(weight, "yl")
    other_rows = swap(own_rows, "c")
    passed, crossing, other_rows, queries, grad_out = lax.optimization_barrier(
        (far[0], near[2], other_rows, queries[0], grad_out[0])
    )
    crossed_heads = swap(
        jnp.concatenate([head_part(queries, 1 - core), head_part(grad_out, 1 - core)], axis=0), "c"
    )
    query_rows = [head_part(queries, core), crossed_heads[:half]]
    grad_rows = [head_part(grad_out, core), crossed_heads[half:]]
    far[1] = shift(passed, "x", span, 1)
    far[3] = shift(passed, "x", span, 3)
    far[2] = swap(crossing, "yl")

    def by_block(pair):
        stacked = jnp.concatenate(pair, axis=0).reshape(4, BLK, QPG, HD)
        natural = stacked.transpose(0, 2, 1, 3).reshape(4, WIDE, HD)
        turned = stacked.transpose(0, 3, 2, 1).reshape(4, HD, WIDE)
        return natural, turned

    q_n, q_t = by_block(query_rows)
    g_n, g_t = by_block(grad_rows)

    def block_places(plane_index):
        first = plane_index % planes * 4
        mine = lax.dynamic_slice_in_dim(block_order, first + 2 * core, 2)
        others = lax.dynamic_slice_in_dim(block_order, first + 2 * (1 - core), 2)
        return jnp.concatenate([mine, others])

    qpos = block_places(plane)
    none = jnp.full((4,), 1 << 20, jnp.int32)
    kpos = jnp.stack(
        [jnp.concatenate([qpos, none])]
        + [
            jnp.concatenate([block_places(plane + k), block_places(plane + planes - k)])
            for k in range(1, 4)
        ]
        + [jnp.concatenate([block_places(plane + 4), none])]
    )
    ids = jnp.arange(8, dtype=jnp.int32)
    mine_at, other_at = kpos[:, :, None], kpos[:, None, :]
    lower = (other_at < mine_at) | ((other_at == mine_at) & (ids[None, None, :] < ids[None, :, None]))
    rank = jnp.sum(lower.astype(jnp.int32), axis=2)
    order = jnp.sum(
        jnp.where(rank[:, :, None] == ids[None, None, :], ids[None, :, None], 0), axis=1
    )
    counts = jnp.sum((kpos[:, None, :] < qpos[None, :, None]).astype(jnp.int32), axis=2)
    plan = (counts, order)

    rows = jnp.concatenate([own_rows, other_rows], axis=0)
    total = None
    for here, parts, order in (
        (side, near, (0, 1, 3, 2)),
        (1 - side, far, (0, 1, 3, 2)),
    ):
        for k in order:
            source = here * span + (place + span - k) % span
            term = nn(columns(rows, source * depth, depth), parts[k])
            total = term if total is None else total + term
    kv = total.astype(BF16)

    rights, lefts = [kv], [kv]
    for k in range(1, 4):
        rights.append(shift(rights[-1], "z", planes, 1))
        lefts.append(shift(lefts[-1], "z", planes, -1))
    rights.append(shift(rights[-1][:half], "z", planes, 1))
    lefts.append(shift(lefts[-1][half:], "z", planes, -1))

    state = row_stats(0, plan, q_t, g_t, [kv], [], False)
    for k in range(1, 4):
        state = row_stats(k, plan, q_t, g_t, [lefts[k], rights[k]], state, False)
        if k == 1:
            near_state = state
    lse, delta, *_ = row_stats(4, plan, q_t, g_t, [rights[4], lefts[4]], state, True)

    by_place = jnp.concatenate(
        [
            columns(own_rows, which * stretch + i * depth, depth)
            for i in range(span)
            for which in (1 - side, side)
        ],
        axis=0,
    )
    latents_x = lax.all_to_all(after(by_place, near_state[1]), "x", 0, 0, tiled=True)
    latents_other = swap(latents_x, "c")

    grads = partial(
        kv_grads, plan=plan, q_t=q_t, g_t=g_t, q_n=q_n, g_n=g_n, lse=lse, delta=delta
    )
    distant = grads(4, [rights[4], lefts[4]])
    to_right = shift(distant[:half].astype(BF16), "z", planes, 1)
    to_left = shift(distant[half:].astype(BF16), "z", planes, -1)
    def half_of(which, *late):
        held = lax.optimization_barrier((*near, *far, *late))
        chosen = [
            jnp.where(which == side, a, b) for a, b in zip(held[:span], held[span : 2 * span])
        ]
        turned = [pick(chosen, (place + span - i) % span) for i in range(span)]
        return jnp.concatenate(turned, axis=0)

    group_w = swap(half_of(1 - group, distant), "t")
    core_group_w = swap(group_w, "c")

    for k in range(3, 0, -1):
        pair = grads(k, [lefts[k], rights[k]])
        ahead, behind = pair[: 2 * half], pair[2 * half :]
        if k == 3:
            ahead = jnp.concatenate([ahead[:half] + to_right.astype(F32), ahead[half:]], axis=0)
            behind = jnp.concatenate([behind[:half], behind[half:] + to_left.astype(F32)], axis=0)
        else:
            ahead = ahead + to_right.astype(F32)
            behind = behind + to_left.astype(F32)
        to_right = shift(ahead.astype(BF16), "z", planes, 1)
        to_left = shift(behind.astype(BF16), "z", planes, -1)
    kv_last, latents_x, latents_other = lax.optimization_barrier((kv, latents_x, latents_other))
    here = grads(0, [kv_last])
    grad_kv = (here + to_right.astype(F32) + to_left.astype(F32)).astype(BF16)

    gathered = [grad_kv] + [shift(grad_kv, "x", span, k) for k in range(1, span)]
    grad_group = swap(grad_kv, "t")
    mine_w = half_of(group, grad_kv)
    core_w = swap(mine_w, "c")

    def weight_term(which):
        return weight_grads(
            jnp.reshape(place, (1,)), which, latents_x, latents_other, gathered
        )

    crossed = swap(weight_term(0).astype(BF16), "yl")
    weight_grad = (weight_term(1) + crossed.astype(F32)).astype(BF16)
    cut = depth // planes
    spread = lax.all_to_all(weight_grad.reshape(planes, cut, 2 * HD), "z", 0, 0, tiled=True)
    summed = jnp.sum(spread.astype(F32), axis=0).astype(BF16)
    copies = jnp.broadcast_to(summed[None], (2 * planes, cut, 2 * HD))
    whole = lax.all_to_all(copies, ("z", "c"), 0, 0, tiled=True)
    whole = whole.reshape(planes, 2, cut, 2 * HD).transpose(0, 2, 1, 3).astype(F32)
    key_out = whole[..., :HD].reshape(depth, 2 * HD)
    value_out = whole[..., HD:].reshape(depth, 2 * HD)

    grad_core = swap(grad_kv[half:], "c")
    grad_core_group = swap(grad_group[half:], "c")
    grad_inputs = (
        dot_nt(grad_kv[:half], mine_w)
        + dot_nt(grad_core, core_w)
        + dot_nt(grad_group[:half], group_w)
        + dot_nt(grad_core_group, core_group_w)
    ).astype(BF16)
    return grad_inputs[None], key_out, value_out


def solution(mesh):
    sizes = mesh.shape
    ctx, fsdp, tp = sizes["ctx"], sizes["fsdp"], sizes["tp"]
    fine = Mesh(
        mesh.devices.reshape(ctx // 2, 2, 2, fsdp // 2, tp), ("z", "c", "yl", "x", "t")
    )
    rows, cols = ("z", "c"), ("yl", "x")
    placed = (
        P(cols, rows, None),
        P(cols, rows, "t"),
        P(cols, rows, "t"),
        P(cols, "t"),
        P(cols, "t"),
        P(),
    )
    return jax.shard_map(
        per_device,
        mesh=fine,
        in_specs=placed,
        out_specs=(P(cols, rows, "t"), P(cols, "t"), P(cols, "t")),
        check_vma=False,
    )
```

```python
import math
from functools import partial

import jax
import jax.numpy as jnp
from jax import lax
from jax.experimental import pallas as pl
from jax.experimental.pallas import tpu as pltpu
from jax.sharding import Mesh, PartitionSpec as P

HD = 128
QPG = 5
BLK = 128
WIDE = QPG * BLK
SCALE = HD**-0.5
SCALE2 = SCALE * math.log2(math.e)
LOW = -1e30
VMEM = 20 * 1024 * 1024

F32 = jnp.float32
BF16 = jnp.bfloat16


def nn(a, b):
    return lax.dot_general(a, b, (((1,), (0,)), ((), ())), preferred_element_type=F32)


def dot_tn(a, b):
    return lax.dot_general(a, b, (((0,), (0,)), ((), ())), preferred_element_type=F32)


def causal_mask():
    row = lax.broadcasted_iota(jnp.int32, (BLK, WIDE), 0)
    col = lax.broadcasted_iota(jnp.int32, (BLK, WIDE), 1)
    return row <= col % BLK


def block_at(index):
    return pl.ds(pl.multiple_of(index * BLK, BLK), BLK)


def gather_segments(segments, held):
    base = 0
    for seg in segments:
        held[base : base + seg.shape[0], :] = seg[...]
        base += seg.shape[0]


def heads_of(rows, qb):
    block = slice(qb * BLK, (qb + 1) * BLK)
    return jnp.concatenate([rows[block, h * HD : (h + 1) * HD] for h in range(QPG)], axis=0)


def rows_of(held, blocks, first):
    parts = [held[block_at(b), first : first + HD] for b in blocks]
    return parts[0] if len(parts) == 1 else jnp.concatenate(parts, axis=0)


def walk(counts, order, stage, qb, add):
    visible = counts[stage, qb]
    fours = visible // 4
    left = visible - fours * 4

    def step(i, carry):
        add([order[stage, i * 4 + j] for j in range(4)])
        return carry

    lax.fori_loop(0, fours, step, 0)

    @pl.when(left >= 2)
    def _():
        add([order[stage, fours * 4 + j] for j in range(2)])

    @pl.when(left % 2 == 1)
    def _():
        add([order[stage, visible - 1]])


def stats_kernel(stage, count, last, *refs):
    counts, order, q_t, g_t = refs[:4]
    segments = refs[4 : 4 + count]
    rest = refs[4 + count :]
    held = rest[-1]
    first = stage == 0
    before, rest = (None, rest[:-1]) if first else (rest[0], rest[1:-1])
    top, total, weighted = [rest[-1].at[i] for i in range(3)]
    gather_segments(segments, held)
    for i, fill in enumerate((LOW, 0.0, 0.0)):
        rest[-1][i] = jnp.full((4, 8, WIDE), fill, F32) if first else before[i]

    for qb in range(4):

        def add(blocks, diagonal=False, qb=qb):
            deep = len(blocks) * BLK // 8
            logits = nn(rows_of(held, blocks, 0), q_t[qb])
            prob_grad = nn(rows_of(held, blocks, HD), g_t[qb])
            if diagonal:
                seen = causal_mask()
                logits = jnp.where(seen, logits, LOW)
            logits = logits.reshape(deep, 8, WIDE)
            prob_grad = prob_grad.reshape(deep, 8, WIDE)
            old = top[qb]
            new = jnp.maximum(old, jnp.max(logits, axis=0))
            weights = jnp.exp2(logits * SCALE2 - (new * SCALE2)[None])
            if diagonal:
                weights = jnp.where(seen.reshape(deep, 8, WIDE), weights, 0.0)
            rescale = jnp.exp2((old - new) * SCALE2)
            top[qb] = new
            total[qb] = total[qb] * rescale + jnp.sum(weights, axis=0)
            weighted[qb] = weighted[qb] * rescale + jnp.sum(weights * prob_grad, axis=0)

        walk(counts, order, stage, qb, add)
        if first:
            add([qb], True)
        if last:
            lse_ref, delta_ref = rest[:2]
            peak = jnp.max(top[qb], axis=0, keepdims=True)
            factor = jnp.exp2((top[qb] - peak) * SCALE2)
            full = jnp.sum(total[qb] * factor, axis=0, keepdims=True)
            lse_ref[qb] = peak * SCALE2 + jnp.log2(full)
            delta_ref[qb] = jnp.sum(weighted[qb] * factor, axis=0, keepdims=True) / full


def grads_kernel(stage, count, *refs):
    counts, order, q_t, g_t, q_n, g_n, lse_ref, delta_ref = refs[:8]
    segments = refs[8 : 8 + count]
    out, held = refs[8 + count :]
    gather_segments(segments, held)
    out[...] = jnp.zeros(out.shape, F32)

    for qb in range(4):

        def add(blocks, diagonal=False, qb=qb):
            logits = nn(rows_of(held, blocks, 0), q_t[qb])
            prob_grad = nn(rows_of(held, blocks, HD), g_t[qb])
            softmax = jnp.exp2(logits * SCALE2 - lse_ref[qb])
            if diagonal:
                softmax = jnp.where(causal_mask(), softmax, 0.0)
            score_grad = (softmax * (prob_grad - delta_ref[qb])).astype(BF16)
            key_grad = nn(score_grad, heads_of(q_n, qb)) * SCALE
            value_grad = nn(softmax.astype(BF16), heads_of(g_n, qb))
            for i, b in enumerate(blocks):
                out[block_at(b), :HD] += key_grad[i * BLK : (i + 1) * BLK]
                out[block_at(b), HD:] += value_grad[i * BLK : (i + 1) * BLK]

        walk(counts, order, stage, qb, add)
        if stage == 0:
            add([qb], True)


def smem():
    return pl.BlockSpec(memory_space=pltpu.SMEM)


def vmem():
    return pl.BlockSpec(memory_space=pltpu.VMEM)


def call(kernel, ins, out_shapes, rows, products, name):
    pairs = rows // BLK * 4 // 2
    return pl.pallas_call(
        kernel,
        out_shape=out_shapes,
        in_specs=[smem(), smem()] + [vmem()] * (len(ins) - 2),
        out_specs=[vmem()] * len(out_shapes),
        scratch_shapes=[pltpu.VMEM((rows, 2 * HD), BF16)],
        compiler_params=pltpu.CompilerParams(vmem_limit_bytes=VMEM),
        cost_estimate=pl.CostEstimate(
            flops=pairs * products * 2 * BLK * WIDE * HD // 4,
            bytes_accessed=rows * 2 * HD * 2,
            transcendentals=0,
        ),
        name=name,
    )(*ins)


def row_stats(stage, plan, q_t, g_t, segments, before, last):
    stat = jax.ShapeDtypeStruct((3, 4, 8, WIDE), F32)
    line = jax.ShapeDtypeStruct((4, 1, WIDE), F32)
    return call(
        partial(stats_kernel, stage, len(segments), last),
        [*plan, q_t, g_t, *segments, *before],
        ([line, line] if last else []) + [stat],
        sum(s.shape[0] for s in segments),
        2,
        "row_stats",
    )


def kv_grads(stage, segments, plan, q_t, g_t, q_n, g_n, lse, delta):
    rows = sum(s.shape[0] for s in segments)
    (out,) = call(
        partial(grads_kernel, stage, len(segments)),
        [*plan, q_t, g_t, q_n, g_n, lse, delta, *segments],
        [jax.ShapeDtypeStruct((rows, 2 * HD), F32)],
        rows,
        4,
        "kv_grads",
    )
    return out


def weight_kernel(place_ref, own, other, *refs):
    gathered, out = refs[:-1], refs[-1]
    span = len(gathered)
    half = gathered[0].shape[0] // 2
    for k, grad in enumerate(gathered):
        source = lax.rem(place_ref[0] + span - k, span)
        term = dot_tn(own[source, 0], grad[:half, :]) + dot_tn(other[source, 0], grad[half:, :])
        if k == 0:
            out[...] = term
        else:
            out[...] += term


def weight_grads(place, which, own, other, gathered):
    span = len(gathered)
    half = gathered[0].shape[0] // 2
    depth = own.shape[1]
    own = own.reshape(span, 2, half, depth)
    other = other.reshape(span, 2, half, depth)
    part = pl.BlockSpec((span, 1, half, depth), lambda i: (0, which, 0, 0))
    grad = pl.BlockSpec(gathered[0].shape, lambda i: (0, 0))
    return pl.pallas_call(
        weight_kernel,
        grid=(1,),
        out_shape=jax.ShapeDtypeStruct((depth, 2 * HD), F32),
        in_specs=[smem(), part, part] + [grad] * span,
        out_specs=pl.BlockSpec((depth, 2 * HD), lambda i: (0, 0)),
        compiler_params=pltpu.CompilerParams(vmem_limit_bytes=VMEM),
        cost_estimate=pl.CostEstimate(
            flops=4 * span * half * depth * 2 * HD,
            bytes_accessed=4 * span * half * depth,
            transcendentals=0,
        ),
        name="weight_grads",
    )(place, own, other, *gathered)


def shift(value, axes, count, by):
    return lax.ppermute(value, axes, [(i, (i + by) % count) for i in range(count)])


def swap(value, axis):
    return lax.ppermute(value, axis, [(0, 1), (1, 0)])


def columns(value, start, width):
    return lax.dynamic_slice_in_dim(value, start, width, 1)


def after(value, *others):
    return lax.optimization_barrier((value, *others))[0]


def pick(parts, index):
    chosen = parts[0]
    for i in range(1, len(parts)):
        chosen = jnp.where(index == i, parts[i], chosen)
    return chosen


def dot_nt(a, b):
    return lax.dot_general(a, b, (((1,), (1,)), ((), ())), preferred_element_type=F32)


def per_device(latents, queries, grad_out, key_weight, value_weight, block_order):
    own_rows = latents[0]
    half = own_rows.shape[0]
    planes = lax.axis_size("z")
    span = lax.axis_size("x")
    core = lax.axis_index("c")
    plane = lax.axis_index("z")
    group = lax.axis_index("t")
    side = lax.axis_index("yl")
    place = lax.axis_index("x")
    depth = key_weight.shape[0]
    stretch = depth * span

    def head_part(value, which):
        return columns(value, which * WIDE, WIDE)

    weight = jnp.concatenate(
        [columns(key_weight, core * HD, HD), columns(value_weight, core * HD, HD)], axis=1
    )
    near, far = [weight] * span, [weight] * span
    for k in (2, 1, 3):
        near[k] = shift(weight, "x", span, k)
    far[0] = swap(weight, "yl")
    other_rows = swap(own_rows, "c")
    passed, crossing, other_rows, queries, grad_out = lax.optimization_barrier(
        (far[0], near[2], other_rows, queries[0], grad_out[0])
    )
    crossed_heads = swap(
        jnp.concatenate([head_part(queries, 1 - core), head_part(grad_out, 1 - core)], axis=0), "c"
    )
    query_rows = [head_part(queries, core), crossed_heads[:half]]
    grad_rows = [head_part(grad_out, core), crossed_heads[half:]]
    far[1] = shift(passed, "x", span, 1)
    far[3] = shift(passed, "x", span, 3)
    far[2] = swap(crossing, "yl")

    def by_block(pair):
        stacked = jnp.concatenate(pair, axis=0)
        turned = stacked.reshape(4, BLK, QPG, HD).transpose(0, 3, 2, 1).reshape(4, HD, WIDE)
        return stacked, turned

    q_n, q_t = by_block(query_rows)
    g_n, g_t = by_block(grad_rows)

    def block_places(plane_index):
        first = plane_index % planes * 4
        mine = lax.dynamic_slice_in_dim(block_order, first + 2 * core, 2)
        others = lax.dynamic_slice_in_dim(block_order, first + 2 * (1 - core), 2)
        return jnp.concatenate([mine, others])

    qpos = block_places(plane)
    none = jnp.full((4,), 1 << 20, jnp.int32)
    kpos = jnp.stack(
        [jnp.concatenate([qpos, none])]
        + [
            jnp.concatenate([block_places(plane + k), block_places(plane + planes - k)])
            for k in range(1, 4)
        ]
        + [jnp.concatenate([block_places(plane + 4), none])]
    )
    ids = jnp.arange(8, dtype=jnp.int32)
    mine_at, other_at = kpos[:, :, None], kpos[:, None, :]
    lower = (other_at < mine_at) | ((other_at == mine_at) & (ids[None, None, :] < ids[None, :, None]))
    rank = jnp.sum(lower.astype(jnp.int32), axis=2)
    order = jnp.sum(
        jnp.where(rank[:, :, None] == ids[None, None, :], ids[None, :, None], 0), axis=1
    )
    counts = jnp.sum((kpos[:, None, :] < qpos[None, :, None]).astype(jnp.int32), axis=2)
    plan = (counts, order)

    rows = jnp.concatenate([own_rows, other_rows], axis=0)
    total = None
    for here, parts, order in (
        (side, near, (0, 1, 3, 2)),
        (1 - side, far, (0, 1, 3, 2)),
    ):
        for k in order:
            source = here * span + (place + span - k) % span
            term = nn(columns(rows, source * depth, depth), parts[k])
            total = term if total is None else total + term
    kv = total.astype(BF16)

    def half_of(which, *late):
        held = lax.optimization_barrier((*near, *far, *late))
        chosen = [
            jnp.where(which == side, a, b) for a, b in zip(held[:span], held[span : 2 * span])
        ]
        turned = [pick(chosen, (place + span - i) % span) for i in range(span)]
        return jnp.concatenate(turned, axis=0)

    rights, lefts = [kv], [kv]
    (state,) = row_stats(0, plan, q_t, g_t, [kv], [], False)
    gates = []
    for k in range(1, 5):
        to_right, to_left = rights[-1], lefts[-1]
        if k == 4:
            to_right, to_left = to_right[:half], to_left[half:]
        if gates:
            to_right, to_left = lax.optimization_barrier((to_right, to_left, *gates))[:2]
        rights.append(shift(to_right, "z", planes, 1))
        lefts.append(shift(to_left, "z", planes, -1))
        if k > 1:
            (state,) = row_stats(
                k - 1, plan, q_t, g_t, [lefts[k - 1], rights[k - 1]], [state], False
            )
        gates = [state]
        if k == 2:
            theirs_w = half_of(1 - group, lefts[2])
        if k == 3:
            gates.append(theirs_w)
    lse, delta, _ = row_stats(4, plan, q_t, g_t, [rights[4], lefts[4]], [state], True)
    group_w = swap(theirs_w, "t")
    core_group_w = swap(group_w, "c")

    by_place = jnp.concatenate(
        [
            columns(own_rows, which * stretch + i * depth, depth)
            for i in range(span)
            for which in (1 - side, side)
        ],
        axis=0,
    )
    latents_x = lax.all_to_all(after(by_place, lefts[1], rights[1]), "x", 0, 0, tiled=True)
    latents_other = swap(latents_x, "c")

    grads = partial(
        kv_grads, plan=plan, q_t=q_t, g_t=g_t, q_n=q_n, g_n=g_n, lse=lse, delta=delta
    )
    distant = grads(4, [rights[4], lefts[4]])
    to_right = shift(distant[:half].astype(BF16), "z", planes, 1)
    to_left = shift(distant[half:].astype(BF16), "z", planes, -1)
    for k in range(3, 0, -1):
        gate = distant if k == 3 else pair
        segments = lax.optimization_barrier((lefts[k], rights[k], gate))[:2]
        pair = grads(k, list(segments))
        ahead, behind = pair[: 2 * half], pair[2 * half :]
        if k == 3:
            ahead = jnp.concatenate([ahead[:half] + to_right.astype(F32), ahead[half:]], axis=0)
            behind = jnp.concatenate([behind[:half], behind[half:] + to_left.astype(F32)], axis=0)
        else:
            ahead = ahead + to_right.astype(F32)
            behind = behind + to_left.astype(F32)
        to_right = shift(ahead.astype(BF16), "z", planes, 1)
        to_left = shift(behind.astype(BF16), "z", planes, -1)
    kv_last, latents_x, latents_other = lax.optimization_barrier((kv, latents_x, latents_other))
    here = grads(0, [kv_last])
    grad_kv = (here + to_right.astype(F32) + to_left.astype(F32)).astype(BF16)

    gathered = [grad_kv] + [shift(grad_kv, "x", span, k) for k in range(1, span)]
    grad_group = swap(grad_kv, "t")
    mine_w = half_of(group, grad_kv)
    core_w = swap(mine_w, "c")

    def weight_term(which):
        return weight_grads(
            jnp.reshape(place, (1,)), which, latents_x, latents_other, gathered
        )

    crossed = swap(weight_term(0).astype(BF16), "yl")
    weight_grad = (weight_term(1) + crossed.astype(F32)).astype(BF16)
    cut = depth // planes
    spread = lax.all_to_all(weight_grad.reshape(planes, cut, 2 * HD), "z", 0, 0, tiled=True)
    summed = jnp.sum(spread.astype(F32), axis=0).astype(BF16)
    copies = jnp.broadcast_to(summed[None], (2 * planes, cut, 2 * HD))
    whole = lax.all_to_all(copies, ("z", "c"), 0, 0, tiled=True)
    whole = whole.reshape(planes, 2, cut, 2 * HD).transpose(0, 2, 1, 3).astype(F32)
    key_out = whole[..., :HD].reshape(depth, 2 * HD)
    value_out = whole[..., HD:].reshape(depth, 2 * HD)

    grad_core = swap(grad_kv[half:], "c")
    grad_core_group = swap(grad_group[half:], "c")
    grad_inputs = (
        dot_nt(grad_kv[:half], mine_w)
        + dot_nt(grad_core, core_w)
        + dot_nt(grad_group[:half], group_w)
        + dot_nt(grad_core_group, core_group_w)
    ).astype(BF16)
    return grad_inputs[None], key_out, value_out


def solution(mesh):
    sizes = mesh.shape
    ctx, fsdp, tp = sizes["ctx"], sizes["fsdp"], sizes["tp"]
    fine = Mesh(
        mesh.devices.reshape(ctx // 2, 2, 2, fsdp // 2, tp), ("z", "c", "yl", "x", "t")
    )
    rows, cols = ("z", "c"), ("yl", "x")
    placed = (
        P(cols, rows, None),
        P(cols, rows, "t"),
        P(cols, rows, "t"),
        P(cols, "t"),
        P(cols, "t"),
        P(),
    )
    return jax.shard_map(
        per_device,
        mesh=fine,
        in_specs=placed,
        out_specs=(P(cols, rows, "t"), P(cols, "t"), P(cols, "t")),
        check_vma=False,
    )
```

```python
import math
from functools import partial

import jax
import jax.numpy as jnp
from jax import lax
from jax.experimental import pallas as pl
from jax.experimental.pallas import tpu as pltpu
from jax.sharding import Mesh, PartitionSpec as P

HD = 128
QPG = 5
BLK = 128
WIDE = QPG * BLK
SCALE = HD**-0.5
SCALE2 = SCALE * math.log2(math.e)
LOW = -1e30
VMEM = 20 * 1024 * 1024

F32 = jnp.float32
BF16 = jnp.bfloat16


def nn(a, b):
    return lax.dot_general(a, b, (((1,), (0,)), ((), ())), preferred_element_type=F32)


def dot_tn(a, b):
    return lax.dot_general(a, b, (((0,), (0,)), ((), ())), preferred_element_type=F32)


def causal_mask():
    row = lax.broadcasted_iota(jnp.int32, (BLK, WIDE), 0)
    col = lax.broadcasted_iota(jnp.int32, (BLK, WIDE), 1)
    return row <= col % BLK


def block_at(index):
    return pl.ds(pl.multiple_of(index * BLK, BLK), BLK)


def gather_segments(segments, held):
    base = 0
    for seg in segments:
        held[base : base + seg.shape[0], :] = seg[...]
        base += seg.shape[0]


def heads_of(rows, qb):
    block = slice(qb * BLK, (qb + 1) * BLK)
    return jnp.concatenate([rows[block, h * HD : (h + 1) * HD] for h in range(QPG)], axis=0)


def rows_of(held, blocks, first):
    parts = [held[block_at(b), first : first + HD] for b in blocks]
    return parts[0] if len(parts) == 1 else jnp.concatenate(parts, axis=0)


def walk(counts, order, stage, qb, add):
    visible = counts[stage, qb]
    fours = visible // 4
    left = visible - fours * 4

    def step(i, carry):
        add([order[stage, i * 4 + j] for j in range(4)])
        return carry

    lax.fori_loop(0, fours, step, 0)

    @pl.when(left >= 2)
    def _():
        add([order[stage, fours * 4 + j] for j in range(2)])

    @pl.when(left % 2 == 1)
    def _():
        add([order[stage, visible - 1]])


def stats_kernel(stage, count, last, *refs):
    counts, order, q_t, g_t = refs[:4]
    segments = refs[4 : 4 + count]
    rest = refs[4 + count :]
    held = rest[-1]
    first = stage == 0
    before, rest = (None, rest[:-1]) if first else (rest[0], rest[1:-1])
    top, total, weighted = [rest[-1].at[i] for i in range(3)]
    gather_segments(segments, held)
    for i, fill in enumerate((LOW, 0.0, 0.0)):
        rest[-1][i] = jnp.full((4, 8, WIDE), fill, F32) if first else before[i]

    for qb in range(4):

        def add(blocks, diagonal=False, qb=qb):
            deep = len(blocks) * BLK // 8
            logits = nn(rows_of(held, blocks, 0), q_t[qb])
            prob_grad = nn(rows_of(held, blocks, HD), g_t[qb])
            if diagonal:
                seen = causal_mask()
                logits = jnp.where(seen, logits, LOW)
            logits = logits.reshape(deep, 8, WIDE)
            prob_grad = prob_grad.reshape(deep, 8, WIDE)
            old = top[qb]
            new = jnp.maximum(old, jnp.max(logits, axis=0))
            weights = jnp.exp2(logits * SCALE2 - (new * SCALE2)[None])
            if diagonal:
                weights = jnp.where(seen.reshape(deep, 8, WIDE), weights, 0.0)
            rescale = jnp.exp2((old - new) * SCALE2)
            top[qb] = new
            total[qb] = total[qb] * rescale + jnp.sum(weights, axis=0)
            weighted[qb] = weighted[qb] * rescale + jnp.sum(weights * prob_grad, axis=0)

        walk(counts, order, stage, qb, add)
        if first:
            add([qb], True)
        if last:
            lse_ref, delta_ref = rest[:2]
            peak = jnp.max(top[qb], axis=0, keepdims=True)
            factor = jnp.exp2((top[qb] - peak) * SCALE2)
            full = jnp.sum(total[qb] * factor, axis=0, keepdims=True)
            lse_ref[qb] = peak * SCALE2 + jnp.log2(full)
            delta_ref[qb] = jnp.sum(weighted[qb] * factor, axis=0, keepdims=True) / full


def grads_kernel(stage, count, *refs):
    counts, order, q_t, g_t, q_n, g_n, lse_ref, delta_ref = refs[:8]
    segments = refs[8 : 8 + count]
    out, held = refs[8 + count :]
    gather_segments(segments, held)
    out[...] = jnp.zeros(out.shape, F32)

    for qb in range(4):

        def add(blocks, diagonal=False, qb=qb):
            logits = nn(rows_of(held, blocks, 0), q_t[qb])
            prob_grad = nn(rows_of(held, blocks, HD), g_t[qb])
            softmax = jnp.exp2(logits * SCALE2 - lse_ref[qb])
            if diagonal:
                softmax = jnp.where(causal_mask(), softmax, 0.0)
            score_grad = (softmax * (prob_grad - delta_ref[qb])).astype(BF16)
            key_grad = nn(score_grad, heads_of(q_n, qb)) * SCALE
            value_grad = nn(softmax.astype(BF16), heads_of(g_n, qb))
            for i, b in enumerate(blocks):
                out[block_at(b), :HD] += key_grad[i * BLK : (i + 1) * BLK]
                out[block_at(b), HD:] += value_grad[i * BLK : (i + 1) * BLK]

        walk(counts, order, stage, qb, add)
        if stage == 0:
            add([qb], True)


def smem():
    return pl.BlockSpec(memory_space=pltpu.SMEM)


def vmem():
    return pl.BlockSpec(memory_space=pltpu.VMEM)


def call(kernel, ins, out_shapes, rows, products, name):
    pairs = rows // BLK * 4 // 2
    return pl.pallas_call(
        kernel,
        out_shape=out_shapes,
        in_specs=[smem(), smem()] + [vmem()] * (len(ins) - 2),
        out_specs=[vmem()] * len(out_shapes),
        scratch_shapes=[pltpu.VMEM((rows, 2 * HD), BF16)],
        compiler_params=pltpu.CompilerParams(vmem_limit_bytes=VMEM),
        cost_estimate=pl.CostEstimate(
            flops=pairs * products * 2 * BLK * WIDE * HD // 4,
            bytes_accessed=rows * 2 * HD * 2,
            transcendentals=0,
        ),
        name=name,
    )(*ins)


def row_stats(stage, plan, q_t, g_t, segments, before, last):
    stat = jax.ShapeDtypeStruct((3, 4, 8, WIDE), F32)
    line = jax.ShapeDtypeStruct((4, 1, WIDE), F32)
    return call(
        partial(stats_kernel, stage, len(segments), last),
        [*plan, q_t, g_t, *segments, *before],
        ([line, line] if last else []) + [stat],
        sum(s.shape[0] for s in segments),
        2,
        "row_stats",
    )


def kv_grads(stage, segments, plan, q_t, g_t, q_n, g_n, lse, delta):
    rows = sum(s.shape[0] for s in segments)
    (out,) = call(
        partial(grads_kernel, stage, len(segments)),
        [*plan, q_t, g_t, q_n, g_n, lse, delta, *segments],
        [jax.ShapeDtypeStruct((rows, 2 * HD), F32)],
        rows,
        4,
        "kv_grads",
    )
    return out


def weight_kernel(place_ref, own, other, *refs):
    gathered, out = refs[:-1], refs[-1]
    span = len(gathered)
    half = gathered[0].shape[0] // 2
    for k, grad in enumerate(gathered):
        source = lax.rem(place_ref[0] + span - k, span)
        term = dot_tn(own[source, 0], grad[:half, :]) + dot_tn(other[source, 0], grad[half:, :])
        if k == 0:
            out[...] = term
        else:
            out[...] += term


def weight_grads(place, which, own, other, gathered):
    span = len(gathered)
    half = gathered[0].shape[0] // 2
    depth = own.shape[1]
    own = own.reshape(span, 2, half, depth)
    other = other.reshape(span, 2, half, depth)
    part = pl.BlockSpec((span, 1, half, depth), lambda i: (0, which, 0, 0))
    grad = pl.BlockSpec(gathered[0].shape, lambda i: (0, 0))
    return pl.pallas_call(
        weight_kernel,
        grid=(1,),
        out_shape=jax.ShapeDtypeStruct((depth, 2 * HD), F32),
        in_specs=[smem(), part, part] + [grad] * span,
        out_specs=pl.BlockSpec((depth, 2 * HD), lambda i: (0, 0)),
        compiler_params=pltpu.CompilerParams(vmem_limit_bytes=VMEM),
        cost_estimate=pl.CostEstimate(
            flops=4 * span * half * depth * 2 * HD,
            bytes_accessed=4 * span * half * depth,
            transcendentals=0,
        ),
        name="weight_grads",
    )(place, own, other, *gathered)


def shift(value, axes, count, by):
    return lax.ppermute(value, axes, [(i, (i + by) % count) for i in range(count)])


def swap(value, axis):
    return lax.ppermute(value, axis, [(0, 1), (1, 0)])


def columns(value, start, width):
    return lax.dynamic_slice_in_dim(value, start, width, 1)


def after(value, *others):
    return lax.optimization_barrier((value, *others))[0]


def pick(parts, index):
    chosen = parts[0]
    for i in range(1, len(parts)):
        chosen = jnp.where(index == i, parts[i], chosen)
    return chosen


def dot_nt(a, b):
    return lax.dot_general(a, b, (((1,), (1,)), ((), ())), preferred_element_type=F32)


def per_device(latents, queries, grad_out, key_weight, value_weight, block_order):
    own_rows = latents[0]
    half = own_rows.shape[0]
    planes = lax.axis_size("z")
    span = lax.axis_size("x")
    core = lax.axis_index("c")
    plane = lax.axis_index("z")
    group = lax.axis_index("t")
    side = lax.axis_index("yl")
    place = lax.axis_index("x")
    depth = key_weight.shape[0]
    stretch = depth * span

    def head_part(value, which):
        return columns(value, which * WIDE, WIDE)

    weight = jnp.concatenate(
        [columns(key_weight, core * HD, HD), columns(value_weight, core * HD, HD)], axis=1
    )
    near, far = [weight] * span, [weight] * span
    for k in (2, 1, 3):
        near[k] = shift(weight, "x", span, k)
    far[0] = swap(weight, "yl")
    other_rows = swap(own_rows, "c")
    passed, crossing, other_rows, queries, grad_out = lax.optimization_barrier(
        (far[0], near[2], other_rows, queries[0], grad_out[0])
    )
    crossed_heads = swap(
        jnp.concatenate([head_part(queries, 1 - core), head_part(grad_out, 1 - core)], axis=0), "c"
    )
    query_rows = [head_part(queries, core), crossed_heads[:half]]
    grad_rows = [head_part(grad_out, core), crossed_heads[half:]]
    far[1] = shift(passed, "x", span, 1)
    far[3] = shift(passed, "x", span, 3)
    far[2] = swap(crossing, "yl")

    def by_block(pair):
        stacked = jnp.concatenate(pair, axis=0)
        turned = stacked.reshape(4, BLK, QPG, HD).transpose(0, 3, 2, 1).reshape(4, HD, WIDE)
        return stacked, turned

    q_n, q_t = by_block(query_rows)
    g_n, g_t = by_block(grad_rows)

    def block_places(plane_index):
        first = plane_index % planes * 4
        mine = lax.dynamic_slice_in_dim(block_order, first + 2 * core, 2)
        others = lax.dynamic_slice_in_dim(block_order, first + 2 * (1 - core), 2)
        return jnp.concatenate([mine, others])

    qpos = block_places(plane)
    none = jnp.full((4,), 1 << 20, jnp.int32)
    kpos = jnp.stack(
        [jnp.concatenate([qpos, none])]
        + [
            jnp.concatenate([block_places(plane + k), block_places(plane + planes - k)])
            for k in range(1, 4)
        ]
        + [jnp.concatenate([block_places(plane + 4), none])]
    )
    ids = jnp.arange(8, dtype=jnp.int32)
    mine_at, other_at = kpos[:, :, None], kpos[:, None, :]
    lower = (other_at < mine_at) | ((other_at == mine_at) & (ids[None, None, :] < ids[None, :, None]))
    rank = jnp.sum(lower.astype(jnp.int32), axis=2)
    order = jnp.sum(
        jnp.where(rank[:, :, None] == ids[None, None, :], ids[None, :, None], 0), axis=1
    )
    counts = jnp.sum((kpos[:, None, :] < qpos[None, :, None]).astype(jnp.int32), axis=2)
    plan = (counts, order)

    rows = jnp.concatenate([own_rows, other_rows], axis=0)
    total = None
    for here, parts, order in (
        (side, near, (0, 1, 3, 2)),
        (1 - side, far, (0, 1, 3, 2)),
    ):
        if parts is far:
            total, q_n, g_n, q_t, g_t = lax.optimization_barrier((total, q_n, g_n, q_t, g_t))
        for k in order:
            source = here * span + (place + span - k) % span
            term = nn(columns(rows, source * depth, depth), parts[k])
            total = term if total is None else total + term
    kv = total.astype(BF16)

    def half_of(which, *late):
        held = lax.optimization_barrier((*near, *far, *late))
        chosen = [
            jnp.where(which == side, a, b) for a, b in zip(held[:span], held[span : 2 * span])
        ]
        turned = [pick(chosen, (place + span - i) % span) for i in range(span)]
        return jnp.concatenate(turned, axis=0)

    rights, lefts = [kv], [kv]
    (state,) = row_stats(0, plan, q_t, g_t, [kv], [], False)
    gates = []
    for k in range(1, 5):
        to_right, to_left = rights[-1], lefts[-1]
        if k == 4:
            to_right, to_left = to_right[:half], to_left[half:]
        if gates:
            to_right, to_left = lax.optimization_barrier((to_right, to_left, *gates))[:2]
        rights.append(shift(to_right, "z", planes, 1))
        lefts.append(shift(to_left, "z", planes, -1))
        if k > 1:
            (state,) = row_stats(
                k - 1, plan, q_t, g_t, [lefts[k - 1], rights[k - 1]], [state], False
            )
        gates = [state]
        if k == 2:
            near_state = state
            theirs_w = half_of(1 - group, lefts[2])
        if k == 3:
            gates.append(theirs_w)
    lse, delta, _ = row_stats(4, plan, q_t, g_t, [rights[4], lefts[4]], [state], True)
    group_w = swap(theirs_w, "t")
    core_group_w = swap(group_w, "c")

    by_place = jnp.concatenate(
        [
            columns(own_rows, which * stretch + i * depth, depth)
            for i in range(span)
            for which in (1 - side, side)
        ],
        axis=0,
    )
    latents_x = lax.all_to_all(after(by_place, near_state), "x", 0, 0, tiled=True)
    latents_other = swap(latents_x, "c")

    grads = partial(
        kv_grads, plan=plan, q_t=q_t, g_t=g_t, q_n=q_n, g_n=g_n, lse=lse, delta=delta
    )
    distant = grads(4, [rights[4], lefts[4]])
    to_right = shift(distant[:half].astype(BF16), "z", planes, 1)
    to_left = shift(distant[half:].astype(BF16), "z", planes, -1)
    for k in range(3, 0, -1):
        gate = (distant,) if k == 3 else (pair,) if k == 2 else (pair, group_w)
        segments = lax.optimization_barrier((lefts[k], rights[k], *gate))[:2]
        pair = grads(k, list(segments))
        ahead, behind = pair[: 2 * half], pair[2 * half :]
        if k == 3:
            ahead = jnp.concatenate([ahead[:half] + to_right.astype(F32), ahead[half:]], axis=0)
            behind = jnp.concatenate([behind[:half], behind[half:] + to_left.astype(F32)], axis=0)
        else:
            ahead = ahead + to_right.astype(F32)
            behind = behind + to_left.astype(F32)
        to_right = shift(ahead.astype(BF16), "z", planes, 1)
        to_left = shift(behind.astype(BF16), "z", planes, -1)
    kv_last, latents_x, latents_other, core_group_w = lax.optimization_barrier(
        (kv, latents_x, latents_other, core_group_w)
    )
    here = grads(0, [kv_last])
    grad_kv = (here + to_right.astype(F32) + to_left.astype(F32)).astype(BF16)

    gathered = [grad_kv] + [shift(grad_kv, "x", span, k) for k in range(1, span)]
    grad_group = swap(grad_kv, "t")
    mine_w = half_of(group, grad_kv)
    core_w = swap(mine_w, "c")

    def weight_term(which):
        return weight_grads(
            jnp.reshape(place, (1,)), which, latents_x, latents_other, gathered
        )

    crossed = swap(weight_term(0).astype(BF16), "yl")
    weight_grad = (weight_term(1) + crossed.astype(F32)).astype(BF16)
    cut = depth // planes
    spread = lax.all_to_all(weight_grad.reshape(planes, cut, 2 * HD), "z", 0, 0, tiled=True)
    summed = jnp.sum(spread.astype(F32), axis=0).astype(BF16)
    copies = jnp.broadcast_to(summed[None], (2 * planes, cut, 2 * HD))
    whole = lax.all_to_all(copies, ("z", "c"), 0, 0, tiled=True)
    whole = whole.reshape(planes, 2, cut, 2 * HD).transpose(0, 2, 1, 3).astype(F32)
    key_out = whole[..., :HD].reshape(depth, 2 * HD)
    value_out = whole[..., HD:].reshape(depth, 2 * HD)

    grad_core = swap(grad_kv[half:], "c")
    grad_core_group = swap(grad_group[half:], "c")
    grad_inputs = (
        dot_nt(grad_kv[:half], mine_w)
        + dot_nt(grad_core, core_w)
        + dot_nt(grad_group[:half], group_w)
        + dot_nt(grad_core_group, core_group_w)
    ).astype(BF16)
    return grad_inputs[None], key_out, value_out


def solution(mesh):
    sizes = mesh.shape
    ctx, fsdp, tp = sizes["ctx"], sizes["fsdp"], sizes["tp"]
    fine = Mesh(
        mesh.devices.reshape(ctx // 2, 2, 2, fsdp // 2, tp), ("z", "c", "yl", "x", "t")
    )
    rows, cols = ("z", "c"), ("yl", "x")
    placed = (
        P(cols, rows, None),
        P(cols, rows, "t"),
        P(cols, rows, "t"),
        P(cols, "t"),
        P(cols, "t"),
        P(),
    )
    return jax.shard_map(
        per_device,
        mesh=fine,
        in_specs=placed,
        out_specs=(P(cols, rows, "t"), P(cols, "t"), P(cols, "t")),
        check_vma=False,
    )
```

```python
import math
from functools import partial

import jax
import jax.numpy as jnp
from jax import lax
from jax.experimental import pallas as pl
from jax.experimental.pallas import tpu as pltpu
from jax.sharding import Mesh, PartitionSpec as P

HD = 128
QPG = 5
BLK = 128
WIDE = QPG * BLK
SCALE = HD**-0.5
SCALE2 = SCALE * math.log2(math.e)
LOW = -1e30
VMEM = 20 * 1024 * 1024

F32 = jnp.float32
BF16 = jnp.bfloat16


def nn(a, b):
    return lax.dot_general(a, b, (((1,), (0,)), ((), ())), preferred_element_type=F32)


def dot_tn(a, b):
    return lax.dot_general(a, b, (((0,), (0,)), ((), ())), preferred_element_type=F32)


def causal_mask():
    row = lax.broadcasted_iota(jnp.int32, (BLK, WIDE), 0)
    col = lax.broadcasted_iota(jnp.int32, (BLK, WIDE), 1)
    return row <= col % BLK


def block_at(index):
    return pl.ds(pl.multiple_of(index * BLK, BLK), BLK)


def gather_segments(segments, held):
    base = 0
    for seg in segments:
        held[base : base + seg.shape[0], :] = seg[...]
        base += seg.shape[0]


def heads_of(rows, qb):
    block = slice(qb * BLK, (qb + 1) * BLK)
    return jnp.concatenate([rows[block, h * HD : (h + 1) * HD] for h in range(QPG)], axis=0)


def rows_of(held, blocks, first):
    parts = [held[block_at(b), first : first + HD] for b in blocks]
    return parts[0] if len(parts) == 1 else jnp.concatenate(parts, axis=0)


def walk(counts, order, stage, qb, add):
    visible = counts[stage, qb]
    fours = visible // 4
    left = visible - fours * 4

    def step(i, carry):
        add([order[stage, i * 4 + j] for j in range(4)])
        return carry

    lax.fori_loop(0, fours, step, 0)

    @pl.when(left >= 2)
    def _():
        add([order[stage, fours * 4 + j] for j in range(2)])

    @pl.when(left % 2 == 1)
    def _():
        add([order[stage, visible - 1]])


def stats_kernel(stage, count, last, *refs):
    counts, order, q_t, g_t = refs[:4]
    segments = refs[4 : 4 + count]
    rest = refs[4 + count :]
    held = rest[-1]
    first = stage == 0
    before, rest = (None, rest[:-1]) if first else (rest[0], rest[1:-1])
    top, total, weighted = [rest[-1].at[i] for i in range(3)]
    gather_segments(segments, held)
    for i, fill in enumerate((LOW, 0.0, 0.0)):
        rest[-1][i] = jnp.full((4, 8, WIDE), fill, F32) if first else before[i]

    for qb in range(4):

        def add(blocks, diagonal=False, qb=qb):
            deep = len(blocks) * BLK // 8
            logits = nn(rows_of(held, blocks, 0), q_t[qb])
            prob_grad = nn(rows_of(held, blocks, HD), g_t[qb])
            if diagonal:
                seen = causal_mask()
                logits = jnp.where(seen, logits, LOW)
            logits = logits.reshape(deep, 8, WIDE)
            prob_grad = prob_grad.reshape(deep, 8, WIDE)
            old = top[qb]
            new = jnp.maximum(old, jnp.max(logits, axis=0))
            weights = jnp.exp2(logits * SCALE2 - (new * SCALE2)[None])
            if diagonal:
                weights = jnp.where(seen.reshape(deep, 8, WIDE), weights, 0.0)
            rescale = jnp.exp2((old - new) * SCALE2)
            top[qb] = new
            total[qb] = total[qb] * rescale + jnp.sum(weights, axis=0)
            weighted[qb] = weighted[qb] * rescale + jnp.sum(weights * prob_grad, axis=0)

        walk(counts, order, stage, qb, add)
        if first:
            add([qb], True)
        if last:
            lse_ref, delta_ref = rest[:2]
            peak = jnp.max(top[qb], axis=0, keepdims=True)
            factor = jnp.exp2((top[qb] - peak) * SCALE2)
            full = jnp.sum(total[qb] * factor, axis=0, keepdims=True)
            lse_ref[qb] = peak * SCALE2 + jnp.log2(full)
            delta_ref[qb] = jnp.sum(weighted[qb] * factor, axis=0, keepdims=True) / full


def grads_kernel(stage, count, *refs):
    counts, order, q_t, g_t, q_n, g_n, lse_ref, delta_ref = refs[:8]
    segments = refs[8 : 8 + count]
    out, held = refs[8 + count :]
    gather_segments(segments, held)
    out[...] = jnp.zeros(out.shape, F32)

    for qb in range(4):

        def add(blocks, diagonal=False, qb=qb):
            logits = nn(rows_of(held, blocks, 0), q_t[qb])
            prob_grad = nn(rows_of(held, blocks, HD), g_t[qb])
            softmax = jnp.exp2(logits * SCALE2 - lse_ref[qb])
            if diagonal:
                softmax = jnp.where(causal_mask(), softmax, 0.0)
            score_grad = (softmax * (prob_grad - delta_ref[qb])).astype(BF16)
            key_grad = nn(score_grad, heads_of(q_n, qb)) * SCALE
            value_grad = nn(softmax.astype(BF16), heads_of(g_n, qb))
            for i, b in enumerate(blocks):
                out[block_at(b), :HD] += key_grad[i * BLK : (i + 1) * BLK]
                out[block_at(b), HD:] += value_grad[i * BLK : (i + 1) * BLK]

        walk(counts, order, stage, qb, add)
        if stage == 0:
            add([qb], True)


def smem():
    return pl.BlockSpec(memory_space=pltpu.SMEM)


def vmem():
    return pl.BlockSpec(memory_space=pltpu.VMEM)


def call(kernel, ins, out_shapes, rows, products, name):
    pairs = rows // BLK * 4 // 2
    return pl.pallas_call(
        kernel,
        out_shape=out_shapes,
        in_specs=[smem(), smem()] + [vmem()] * (len(ins) - 2),
        out_specs=[vmem()] * len(out_shapes),
        scratch_shapes=[pltpu.VMEM((rows, 2 * HD), BF16)],
        compiler_params=pltpu.CompilerParams(vmem_limit_bytes=VMEM),
        cost_estimate=pl.CostEstimate(
            flops=pairs * products * 2 * BLK * WIDE * HD // 4,
            bytes_accessed=rows * 2 * HD * 2,
            transcendentals=0,
        ),
        name=name,
    )(*ins)


def row_stats(stage, plan, q_t, g_t, segments, before, last):
    stat = jax.ShapeDtypeStruct((3, 4, 8, WIDE), F32)
    line = jax.ShapeDtypeStruct((4, 1, WIDE), F32)
    return call(
        partial(stats_kernel, stage, len(segments), last),
        [*plan, q_t, g_t, *segments, *before],
        ([line, line] if last else []) + [stat],
        sum(s.shape[0] for s in segments),
        2,
        "row_stats",
    )


def kv_grads(stage, segments, plan, q_t, g_t, q_n, g_n, lse, delta):
    rows = sum(s.shape[0] for s in segments)
    (out,) = call(
        partial(grads_kernel, stage, len(segments)),
        [*plan, q_t, g_t, q_n, g_n, lse, delta, *segments],
        [jax.ShapeDtypeStruct((rows, 2 * HD), F32)],
        rows,
        4,
        "kv_grads",
    )
    return out


def weight_kernel(place_ref, own, other, *refs):
    gathered, out = refs[:-1], refs[-1]
    span = len(gathered)
    half = gathered[0].shape[0] // 2
    for k, grad in enumerate(gathered):
        source = lax.rem(place_ref[0] + span - k, span)
        term = dot_tn(own[source, 0], grad[:half, :]) + dot_tn(other[source, 0], grad[half:, :])
        if k == 0:
            out[...] = term
        else:
            out[...] += term


def weight_grads(place, which, own, other, gathered):
    span = len(gathered)
    half = gathered[0].shape[0] // 2
    depth = own.shape[1]
    own = own.reshape(span, 2, half, depth)
    other = other.reshape(span, 2, half, depth)
    part = pl.BlockSpec((span, 1, half, depth), lambda i: (0, which, 0, 0))
    grad = pl.BlockSpec(gathered[0].shape, lambda i: (0, 0))
    return pl.pallas_call(
        weight_kernel,
        grid=(1,),
        out_shape=jax.ShapeDtypeStruct((depth, 2 * HD), F32),
        in_specs=[smem(), part, part] + [grad] * span,
        out_specs=pl.BlockSpec((depth, 2 * HD), lambda i: (0, 0)),
        compiler_params=pltpu.CompilerParams(vmem_limit_bytes=VMEM),
        cost_estimate=pl.CostEstimate(
            flops=4 * span * half * depth * 2 * HD,
            bytes_accessed=4 * span * half * depth,
            transcendentals=0,
        ),
        name="weight_grads",
    )(place, own, other, *gathered)


def shift(value, axes, count, by):
    return lax.ppermute(value, axes, [(i, (i + by) % count) for i in range(count)])


def swap(value, axis):
    return lax.ppermute(value, axis, [(0, 1), (1, 0)])


def columns(value, start, width):
    return lax.dynamic_slice_in_dim(value, start, width, 1)


def after(value, *others):
    return lax.optimization_barrier((value, *others))[0]


def pick(parts, index):
    chosen = parts[0]
    for i in range(1, len(parts)):
        chosen = jnp.where(index == i, parts[i], chosen)
    return chosen


def dot_nt(a, b):
    return lax.dot_general(a, b, (((1,), (1,)), ((), ())), preferred_element_type=F32)


def per_device(latents, queries, grad_out, key_weight, value_weight, block_order):
    own_rows = latents[0]
    half = own_rows.shape[0]
    planes = lax.axis_size("z")
    span = lax.axis_size("x")
    core = lax.axis_index("c")
    plane = lax.axis_index("z")
    group = lax.axis_index("t")
    side = lax.axis_index("yl")
    place = lax.axis_index("x")
    depth = key_weight.shape[0]
    stretch = depth * span

    def head_part(value, which):
        return columns(value, which * WIDE, WIDE)

    weight = jnp.concatenate(
        [columns(key_weight, core * HD, HD), columns(value_weight, core * HD, HD)], axis=1
    )
    near, far = [weight] * span, [weight] * span
    for k in (2, 1, 3):
        near[k] = shift(weight, "x", span, k)
    far[0] = swap(weight, "yl")
    other_rows = swap(own_rows, "c")
    passed, crossing, other_rows, queries, grad_out = lax.optimization_barrier(
        (far[0], near[2], other_rows, queries[0], grad_out[0])
    )
    crossed_heads = swap(
        jnp.concatenate([head_part(queries, 1 - core), head_part(grad_out, 1 - core)], axis=0), "c"
    )
    query_rows = [head_part(queries, core), crossed_heads[:half]]
    grad_rows = [head_part(grad_out, core), crossed_heads[half:]]
    far[1] = shift(passed, "x", span, 1)
    far[3] = shift(passed, "x", span, 3)
    far[2] = swap(crossing, "yl")

    def by_block(pair):
        stacked = jnp.concatenate(pair, axis=0)
        turned = stacked.reshape(4, BLK, QPG, HD).transpose(0, 3, 2, 1).reshape(4, HD, WIDE)
        return stacked, turned

    q_n, q_t = by_block(query_rows)
    g_n, g_t = by_block(grad_rows)

    def block_places(plane_index):
        first = plane_index % planes * 4
        mine = lax.dynamic_slice_in_dim(block_order, first + 2 * core, 2)
        others = lax.dynamic_slice_in_dim(block_order, first + 2 * (1 - core), 2)
        return jnp.concatenate([mine, others])

    qpos = block_places(plane)
    none = jnp.full((4,), 1 << 20, jnp.int32)
    kpos = jnp.stack(
        [jnp.concatenate([qpos, none])]
        + [
            jnp.concatenate([block_places(plane + k), block_places(plane + planes - k)])
            for k in range(1, 4)
        ]
        + [jnp.concatenate([block_places(plane + 4), none])]
    )
    ids = jnp.arange(8, dtype=jnp.int32)
    mine_at, other_at = kpos[:, :, None], kpos[:, None, :]
    lower = (other_at < mine_at) | ((other_at == mine_at) & (ids[None, None, :] < ids[None, :, None]))
    rank = jnp.sum(lower.astype(jnp.int32), axis=2)
    order = jnp.sum(
        jnp.where(rank[:, :, None] == ids[None, None, :], ids[None, :, None], 0), axis=1
    )
    counts = jnp.sum((kpos[:, None, :] < qpos[None, :, None]).astype(jnp.int32), axis=2)
    plan = (counts, order)

    rows = jnp.concatenate([own_rows, other_rows], axis=0)
    total = None
    for here, parts, order in (
        (side, near, (0, 1, 3, 2)),
        (1 - side, far, (0, 1, 3, 2)),
    ):
        if parts is far:
            total, q_n, g_n, q_t, g_t = lax.optimization_barrier((total, q_n, g_n, q_t, g_t))
        for k in order:
            source = here * span + (place + span - k) % span
            term = nn(columns(rows, source * depth, depth), parts[k])
            total = term if total is None else total + term
    kv = total.astype(BF16)

    def half_of(which, *late):
        held = lax.optimization_barrier((*near, *far, *late))
        chosen = [
            jnp.where(which == side, a, b) for a, b in zip(held[:span], held[span : 2 * span])
        ]
        turned = [pick(chosen, (place + span - i) % span) for i in range(span)]
        return jnp.concatenate(turned, axis=0)

    rights, lefts = [kv], [kv]
    (state,) = row_stats(0, plan, q_t, g_t, [kv], [], False)
    gates = []
    for k in range(1, 5):
        to_right, to_left = rights[-1], lefts[-1]
        if k == 4:
            to_right, to_left = to_right[:half], to_left[half:]
        if gates:
            to_right, to_left = lax.optimization_barrier((to_right, to_left, *gates))[:2]
        rights.append(shift(to_right, "z", planes, 1))
        lefts.append(shift(to_left, "z", planes, -1))
        if k > 1:
            (state,) = row_stats(
                k - 1, plan, q_t, g_t, [lefts[k - 1], rights[k - 1]], [state], False
            )
        gates = [state]
        if k == 2:
            theirs_w = half_of(1 - group, lefts[2])
        if k == 3:
            near_state = state
            gates.append(theirs_w)
    lse, delta, _ = row_stats(4, plan, q_t, g_t, [rights[4], lefts[4]], [state], True)
    group_w = swap(theirs_w, "t")
    core_group_w = swap(group_w, "c")

    by_place = jnp.concatenate(
        [
            columns(own_rows, which * stretch + i * depth, depth)
            for i in range(span)
            for which in (1 - side, side)
        ],
        axis=0,
    )
    latents_x = lax.all_to_all(after(by_place, near_state), "x", 0, 0, tiled=True)

    grads = partial(
        kv_grads, plan=plan, q_t=q_t, g_t=g_t, q_n=q_n, g_n=g_n, lse=lse, delta=delta
    )
    distant = grads(4, [rights[4], lefts[4]])
    to_right = shift(distant[:half].astype(BF16), "z", planes, 1)
    to_left = shift(distant[half:].astype(BF16), "z", planes, -1)
    for k in range(3, 0, -1):
        gate = (distant,) if k == 3 else (pair,) if k == 2 else (pair, group_w)
        segments = lax.optimization_barrier((lefts[k], rights[k], *gate))[:2]
        pair = grads(k, list(segments))
        if k == 2:
            latents_other = swap(after(latents_x, pair), "c")
        ahead, behind = pair[: 2 * half], pair[2 * half :]
        if k == 3:
            ahead = jnp.concatenate([ahead[:half] + to_right.astype(F32), ahead[half:]], axis=0)
            behind = jnp.concatenate([behind[:half], behind[half:] + to_left.astype(F32)], axis=0)
        else:
            ahead = ahead + to_right.astype(F32)
            behind = behind + to_left.astype(F32)
        to_right = shift(ahead.astype(BF16), "z", planes, 1)
        to_left = shift(behind.astype(BF16), "z", planes, -1)
    kv_last, latents_x, latents_other, core_group_w = lax.optimization_barrier(
        (kv, latents_x, latents_other, core_group_w)
    )
    here = grads(0, [kv_last])
    grad_kv = (here + to_right.astype(F32) + to_left.astype(F32)).astype(BF16)

    gathered = [grad_kv] + [shift(grad_kv, "x", span, k) for k in range(1, span)]
    grad_group = swap(grad_kv, "t")
    mine_w = half_of(group, grad_kv)
    core_w = swap(mine_w, "c")

    def weight_term(which):
        return weight_grads(
            jnp.reshape(place, (1,)), which, latents_x, latents_other, gathered
        )

    crossed = swap(weight_term(0).astype(BF16), "yl")
    weight_grad = (weight_term(1) + crossed.astype(F32)).astype(BF16)
    cut = depth // planes
    spread = lax.all_to_all(weight_grad.reshape(planes, cut, 2 * HD), "z", 0, 0, tiled=True)
    summed = jnp.sum(spread.astype(F32), axis=0).astype(BF16)
    copies = jnp.broadcast_to(summed[None], (2 * planes, cut, 2 * HD))
    whole = lax.all_to_all(copies, ("z", "c"), 0, 0, tiled=True)
    whole = whole.reshape(planes, 2, cut, 2 * HD).transpose(0, 2, 1, 3).astype(F32)
    key_out = whole[..., :HD].reshape(depth, 2 * HD)
    value_out = whole[..., HD:].reshape(depth, 2 * HD)

    grad_core = swap(grad_kv[half:], "c")
    grad_core_group = swap(grad_group[half:], "c")
    grad_inputs = (
        dot_nt(grad_kv[:half], mine_w)
        + dot_nt(grad_core, core_w)
        + dot_nt(grad_group[:half], group_w)
        + dot_nt(grad_core_group, core_group_w)
    ).astype(BF16)
    return grad_inputs[None], key_out, value_out


def solution(mesh):
    sizes = mesh.shape
    ctx, fsdp, tp = sizes["ctx"], sizes["fsdp"], sizes["tp"]
    fine = Mesh(
        mesh.devices.reshape(ctx // 2, 2, 2, fsdp // 2, tp), ("z", "c", "yl", "x", "t")
    )
    rows, cols = ("z", "c"), ("yl", "x")
    placed = (
        P(cols, rows, None),
        P(cols, rows, "t"),
        P(cols, rows, "t"),
        P(cols, "t"),
        P(cols, "t"),
        P(),
    )
    return jax.shard_map(
        per_device,
        mesh=fine,
        in_specs=placed,
        out_specs=(P(cols, rows, "t"), P(cols, "t"), P(cols, "t")),
        check_vma=False,
    )
```
